32 devices in a mesh: dp: 8 (over z, y), tensor: 4 (over x, core).
Axes of the slice: x: 2, y: 2, z: 4, core: 2. Of those that a mesh axis runs over, the one named last changes fastest.
Arguments:
- x_in: bfloat16 [8, 1024, 1536], P(None, 'dp'), may hold values from -6 to 6
- cotangent: bfloat16 [8, 1024, 1536], P('dp'), may hold values from -6 to 6
- lengths: int32 [8], replicated, may hold values from 128 to 1024, as said below
- deal_order: int32 [8], replicated, may hold values from 0 to 7, each once
- norm_gains: float32 [3, 1536], replicated, may hold values from 0.1 to 1.9
- proj_gate: bfloat16 [2, 1536, 3072], P(None, None, 'tensor'), may hold values from -0.15625 to 0.15625
- proj_value: bfloat16 [2, 1536, 3072], P(None, None, 'tensor'), may hold values from -0.15625 to 0.15625
- proj_state: bfloat16 [2, 1536, 256], replicated, may hold values from -0.15625 to 0.15625
- proj_step: bfloat16 [2, 1536, 48], P(None, None, 'tensor'), may hold values from -0.15625 to 0.15625
- proj_out: bfloat16 [2, 1536, 3072], P(None, None, 'tensor'), may hold values from -0.109375 to 0.109375
- conv_value: float32 [2, 5, 3072], P(None, None, 'tensor'), may hold values from -0.5 to 0.5
- conv_state: float32 [2, 5, 256], replicated, may hold values from -0.5 to 0.5
- step_bias: float32 [2, 48], P(None, 'tensor'), may hold values from -7 to -2
- decay_log: float32 [2, 48], P(None, 'tensor'), may hold values from -0.7 to 2.8
- skip_gain: float32 [2, 48], P(None, 'tensor'), may hold values from 0.5 to 1.5
- inner_gain: float32 [2, 3072], P(None, 'tensor'), may hold values from 0.1 to 1.9
Outputs:
- result: bfloat16 [8, 1024, 1536], P('dp')
- grad_x_in: bfloat16 [8, 1024, 1536], P(None, 'dp')
- grad_norm_gains: float32 [3, 1536], P(None, 'dp')
- grad_proj_gate: float32 [2, 1536, 3072], P(None, 'dp', 'tensor')
- grad_proj_value: float32 [2, 1536, 3072], P(None, 'dp', 'tensor')
- grad_proj_state: float32 [2, 1536, 256], P(None, 'dp')
- grad_proj_step: float32 [2, 1536, 48], P(None, 'dp', 'tensor')
- grad_proj_out: float32 [2, 1536, 3072], P(None, 'dp', 'tensor')
- grad_conv_value: float32 [2, 5, 3072], P(None, None, 'tensor')
- grad_conv_state: float32 [2, 5, 256], replicated
- grad_step_bias: float32 [2, 48], P(None, 'tensor')
- grad_decay_log: float32 [2, 48], P(None, 'tensor')
- grad_skip_gain: float32 [2, 48], P(None, 'tensor')
- grad_inner_gain: float32 [2, 3072], P(None, 'tensor')
The draws below stay inside these ranges and needn't reach their ends.
Inputs may be any that keep to these rules, and one draw needn't show every extreme that they name: `lengths`: valid tokens of each sequence's slot of 1024; some sequence fills its slot and some has 128. A permutation of the 8 sequences; dealt position s holds sequence deal_order[s], and positions s * 1 onward go to index s of dp.
All inputs are finite; a program needn't handle non-finite values.
Results may differ from the reference program's by a relative error of at most 0.018.
Values may be sent and summed in bfloat16 or wider, within the bound.
No kernel may reach another device: no remote copies, remote signals or barrier semaphores. Data moves between devices by JAX's collectives and lax.ppermute only.
A program may use at most 256 MiB of HBM per device.

```python
import math
import jax
import jax.numpy as jnp
from jax import lax

D = 1536
H = 48
P_SIZE = 64
N = 128
K = 4
Q = 256
L = 2
SLOT = 1024
NSEQ = 8


def draw_lengths(key, part):
    key = jax.random.fold_in(key, 11)
    first_key, second_key = jax.random.split(key)
    drawn = jax.random.randint(first_key, (NSEQ,), SLOT // 8, SLOT + 1)
    picks = jax.random.permutation(second_key, NSEQ)
    drawn = drawn.at[picks[0]].set(SLOT)
    drawn = drawn.at[picks[1]].set(SLOT // 8)
    return drawn.astype(jnp.int32)


def steps_of(own_key, extent, cuts, low, top_value):
    level, own = 1.0, jax.random.fold_in(own_key, 6)
    for axis_at, blocks in cuts:
        heights = jnp.exp(jax.random.uniform(jax.random.fold_in(own, axis_at), (blocks,), jnp.float32, low / len(cuts), top_value / len(cuts)))
        level = level * jnp.repeat(heights, extent[axis_at] // blocks).reshape([-1 if axis == axis_at else 1 for axis in range(len(extent))])
    return level


def centred(stream_key, shape, spread, bound, shards=(), dtype=jnp.bfloat16):
    values = spread * jax.random.normal(stream_key, shape, jnp.float32)
    if shards:
        values = values * steps_of(stream_key, shape, shards, -0.22, 0.18)
    return jnp.clip(values, -bound, bound).astype(dtype)


def setup_inputs(seed: int = 0) -> dict:
    keys = jax.random.split(jax.random.key(seed), 17)
    return {
        "x_in": centred(keys[0], (NSEQ, SLOT, D), 1.0, 6.0, ((1, 8),)),
        "cotangent": centred(keys[1], (NSEQ, SLOT, D), 1.0, 6.0, ((0, 8),)),
        "lengths": draw_lengths(jax.random.fold_in(keys[16], 71), 0),
        "deal_order": jax.random.permutation(keys[3], NSEQ).astype(jnp.int32),
        "norm_gains": jnp.clip(1.0 + 0.18 * jax.random.normal(keys[4], (L + 1, D), jnp.float32), 0.1, 1.9),
        "proj_gate": centred(keys[5], (L, D, H * P_SIZE), D ** -0.5, 0.15625, ((2, 4),)),
        "proj_value": centred(keys[6], (L, D, H * P_SIZE), D ** -0.5, 0.15625, ((2, 4),)),
        "proj_state": centred(keys[7], (L, D, 2 * N), D ** -0.5, 0.15625),
        "proj_step": centred(keys[8], (L, D, H), D ** -0.5, 0.15625, ((2, 4),)),
        "proj_out": centred(keys[9], (L, D, H * P_SIZE), (H * P_SIZE) ** -0.5, 0.109375, ((2, 4),)),
        "conv_value": jnp.clip(jax.random.uniform(keys[10], (L, K + 1, H * P_SIZE), jnp.float32, -0.5, 0.5) * steps_of(keys[10], (L, K + 1, H * P_SIZE), ((2, 4),), -0.4, 0.0), -0.5, 0.5),
        "conv_state": jnp.clip(jax.random.uniform(keys[11], (L, K + 1, 2 * N), jnp.float32, -0.5, 0.5), -0.5, 0.5),
        "step_bias": jnp.clip(-7.0 + 5.0 * jax.random.uniform(keys[12], (L, H), jnp.float32) ** steps_of(keys[12], (L, H), ((1, 4),), -0.2, 0.2), -7.0, -2.0),
        "decay_log": jnp.clip(-0.7 + 3.5 * jax.random.uniform(keys[13], (L, H), jnp.float32) ** steps_of(keys[13], (L, H), ((1, 4),), -0.2, 0.2), -0.7, 2.8),
        "skip_gain": jnp.clip(0.5 + 1.0 * jax.random.uniform(keys[14], (L, H), jnp.float32) ** steps_of(keys[14], (L, H), ((1, 4),), -0.2, 0.2), 0.5, 1.5),
        "inner_gain": jnp.clip(1.0 + 0.18 * jax.random.normal(keys[15], (L, H * P_SIZE), jnp.float32), 0.1, 1.9),
    }


exact_mode = lax.Precision.HIGHEST
eps_norm = 1e-05

@jax.custom_vjp
def low(v):
    return lax.optimization_barrier(v.astype(jnp.bfloat16)).astype(jnp.float32)

@jax.custom_vjp
def low_back(v):
    return v

def low_keep(v):
    return (low(v), None)

def low_pass(kept, grad):
    return (grad,)

def back_keep(v):
    return (v, None)

def back_low(kept, grad):
    return (low(grad),)
low.defvjp(low_keep, low_pass)
low_back.defvjp(back_keep, back_low)

def causal_conv(values, conv_taps):
    tap_count = conv_taps.shape[0] - 1
    padded = jnp.pad(values, ((tap_count - 1, 0), (0, 0)))
    summed = conv_taps[tap_count] + jnp.zeros_like(values)
    for offset in range(tap_count):
        summed = summed + conv_taps[offset] * padded[offset:offset + values.shape[0]]
    return summed

def block_scan(per_head, step_size, decay, state_in, state_out):
    length, head_count, head_size = per_head.shape
    block_count = length // Q
    log_decay = -(step_size * decay[None, :])
    cumulative = jnp.cumsum(log_decay.reshape(block_count, Q, head_count), axis=1)
    scaled_x = (per_head * step_size[:, :, None]).reshape(block_count, Q, head_count, head_size)
    b_blocks = state_in.reshape(block_count, Q, -1)
    c_blocks = state_out.reshape(block_count, Q, -1)
    row_ids = lax.broadcasted_iota(jnp.int32, (Q, Q), 0)
    col_ids = lax.broadcasted_iota(jnp.int32, (Q, Q), 1)
    causal = row_ids >= col_ids
    gaps = cumulative[:, :, None, :] - cumulative[:, None, :, :]
    weights = jnp.exp(jnp.where(causal[None, :, :, None], gaps, -jnp.inf))
    scores = jnp.einsum('cin,cjn->cij', c_blocks, b_blocks, precision=exact_mode)
    within = jnp.einsum('cijh,cjhp->cihp', scores[..., None] * weights, scaled_x, precision=exact_mode)
    to_end = jnp.exp(cumulative[:, -1:, :] - cumulative)
    states = jnp.einsum('cjn,cjhp->chpn', b_blocks, scaled_x * to_end[..., None], precision=exact_mode)
    block_decay = jnp.exp(cumulative[:, -1, :])
    carried = jnp.zeros((head_count, head_size, b_blocks.shape[-1]), jnp.float32)
    entering = []
    for block_at in range(block_count):
        entering.append(carried)
        carried = carried * block_decay[block_at][:, None, None] + states[block_at]
    entering = jnp.stack(entering)
    across = jnp.einsum('cin,chpn->cihp', c_blocks, entering, precision=exact_mode) * jnp.exp(cumulative)[..., None]
    return (within + across).reshape(length, head_count, head_size)

def mixer_inner(gate_in, value_in, state_in, step_in, conv_value, conv_state, step_bias, decay_log, skip_gain):
    values = jax.nn.silu(causal_conv(value_in, conv_value))
    states = jax.nn.silu(causal_conv(state_in, conv_state))
    state_width = states.shape[1] // 2
    step_size = jax.nn.softplus(step_in + step_bias)
    head_count = step_size.shape[1]
    per_head = values.reshape(values.shape[0], head_count, P_SIZE)
    mixed_out = block_scan(per_head, step_size, jnp.exp(decay_log), states[:, :state_width], states[:, state_width:])
    mixed_out = mixed_out + skip_gain[:, None] * per_head
    return mixed_out.reshape(values.shape[0], -1) * jax.nn.silu(gate_in)

def norm_rows(hidden, gain):
    return hidden * lax.rsqrt(lax.optimization_barrier(jnp.mean(hidden * hidden, axis=-1, keepdims=True)) + eps_norm) * gain

def dense(left, right):
    return jnp.dot(left, right, precision=exact_mode, preferred_element_type=jnp.float32)

def one_sequence(params, x_seq, valid_seq):
    norm_gains, proj_gate, proj_value, proj_state, proj_step, proj_out, conv_value, conv_state, step_bias, decay_log, skip_gain, inner_gain = params
    layer_count = proj_gate.shape[0]
    hidden = x_seq * valid_seq[:, None]
    for index_layer in range(layer_count):
        lowered = low(norm_rows(hidden, norm_gains[index_layer]))
        gate_in = low_back(dense(lowered, proj_gate[index_layer]))
        value_in = low_back(dense(lowered, proj_value[index_layer]))
        state_in = low_back(dense(lowered, proj_state[index_layer]))
        step_in = low_back(dense(lowered, proj_step[index_layer]))
        gated = mixer_inner(gate_in, value_in, state_in, step_in, conv_value[index_layer], conv_state[index_layer], step_bias[index_layer], decay_log[index_layer], skip_gain[index_layer])
        gate_out = low(norm_rows(gated, inner_gain[index_layer]))
        branch = low_back(dense(gate_out, proj_out[index_layer].T))
        hidden = hidden + branch
    return norm_rows(hidden, norm_gains[layer_count]) * valid_seq[:, None]

def reference(x_in, cotangent, lengths, deal_order, norm_gains, proj_gate, proj_value, proj_state, proj_step, proj_out, conv_value, conv_state, step_bias, decay_log, skip_gain, inner_gain):
    seq_count, slot_len, model_width = x_in.shape
    dealt_len = jnp.take(lengths, deal_order)
    positions = lax.broadcasted_iota(jnp.int32, (seq_count, slot_len), 1)
    valid = (positions < dealt_len[:, None].astype(jnp.int32)).astype(jnp.float32)
    params = tuple((item.astype(jnp.float32) for item in (norm_gains, proj_gate, proj_value, proj_state, proj_step, proj_out, conv_value, conv_state, step_bias, decay_log, skip_gain, inner_gain)))
    group_size = math.gcd(seq_count, max(1, 4096 // slot_len))

    def forward(params, x_all):
        dealt_x = jnp.take(x_all, deal_order, axis=0).reshape(seq_count // group_size, group_size, slot_len, model_width)
        valid_blocks = valid.reshape(seq_count // group_size, group_size, slot_len)

        def run_block(block_pair):
            return jax.vmap(one_sequence, (None, 0, 0))(params, block_pair[0], block_pair[1])
        outputs = lax.map(jax.checkpoint(run_block), (dealt_x, valid_blocks))
        return outputs.reshape(seq_count, slot_len, model_width)
    outputs, pullback = jax.vjp(forward, params, x_in.astype(jnp.float32))
    grad_params, grad_x = pullback(cotangent.astype(jnp.float32))
    g_gains, g_gate, g_value, g_state, g_step, g_out, g_conv_value, g_conv_state, g_bias, g_decay, g_skip, g_inner = grad_params
    return (outputs.astype(jnp.bfloat16), grad_x.astype(jnp.bfloat16), g_gains, g_gate, g_value, g_state, g_step, g_out, g_conv_value, g_conv_state, g_bias, g_decay, g_skip, g_inner)
```

```python
import functools

import jax
import jax.numpy as jnp
from jax import lax
from jax.experimental import pallas as pl
from jax.experimental.pallas import tpu as pltpu
from jax.sharding import PartitionSpec as P

P_SIZE = 64
Q = 256
GC = 256
HG = GC // P_SIZE
LANES = 128
EPS = 1e-05
CHUNKS_F = 1
CHUNKS_B = 1
VMEM_LIMIT = 56 * 1024 * 1024

F32 = jnp.float32
BF16 = jnp.bfloat16


def nn(a, b):
    return jnp.dot(a, b, preferred_element_type=F32)


def nt(a, b):
    return lax.dot_general(a, b, (((1,), (1,)), ((), ())), preferred_element_type=F32)


def tn(a, b):
    return lax.dot_general(a, b, (((0,), (0,)), ((), ())), preferred_element_type=F32)


def exact(a, b):
    return jnp.dot(a, b, preferred_element_type=F32, precision=lax.Precision.HIGHEST)


def sigmoid(v):
    return 1.0 / (1.0 + jnp.exp(-v))


def softplus(v):
    return jnp.maximum(v, 0.0) + jnp.log1p(jnp.exp(-jnp.abs(v)))


def triangle(lower):
    rows = lax.broadcasted_iota(jnp.int32, (Q, Q), 0)
    cols = lax.broadcasted_iota(jnp.int32, (Q, Q), 1)
    return rows >= cols if lower else cols >= rows


def row_mean(v):
    return jnp.mean(v, axis=1, keepdims=True)


def col_sum(v):
    return jnp.sum(v, axis=0, keepdims=True)


def join_halves(dst, mine, theirs, core, half):
    width = mine.shape[-1]
    for m in range(Q // (2 * half)):
        own = pl.multiple_of(2 * half * m + half * core, 8)
        other = pl.multiple_of(2 * half * m + half * (1 - core), 8)
        dst[pl.ds(own, half), :width] = mine[half * m : half * m + half, :].astype(F32)
        dst[pl.ds(other, half), :width] = theirs[half * m : half * m + half, :].astype(F32)


def split_halves(src, keep, send, core, half):
    width = keep.shape[-1]
    for m in range(Q // (2 * half)):
        own = pl.multiple_of(2 * half * m + half * core, 8)
        keep[half * m : half * m + half, :] = src[pl.ds(own, half), :width].astype(keep.dtype)
        if send is not None:
            other = pl.multiple_of(2 * half * m + half * (1 - core), 8)
            send[half * m : half * m + half, :] = src[pl.ds(other, half), :width].astype(send.dtype)


def spread(per_head):
    lane = lax.broadcasted_iota(jnp.int32, (Q, LANES), 1)
    tiles = []
    for q in range(GC // LANES):
        left = jnp.broadcast_to(per_head[:, 2 * q : 2 * q + 1], (Q, LANES))
        right = jnp.broadcast_to(per_head[:, 2 * q + 1 : 2 * q + 2], (Q, LANES))
        tiles.append(jnp.where(lane < P_SIZE, left, right))
    return jnp.concatenate(tiles, axis=1)


def head_part(tile, parity):
    lane = lax.broadcasted_iota(jnp.int32, tile.shape, 1)
    return jnp.where((lane < P_SIZE) == (parity == 0), tile, jnp.zeros_like(tile))


def gather_heads(acc, cols, group):
    lane = lax.broadcasted_iota(jnp.int32, (cols.shape[0], LANES), 1)
    for j in range(HG):
        tile = head_part(cols[:, (j // 2) * LANES : (j // 2 + 1) * LANES], j % 2)
        total = jnp.sum(tile, axis=1, keepdims=True)
        acc = acc + jnp.where(lane == group * HG + j, total, 0.0)
    return acc


def conv_rows(buf, taps):
    out = taps[4:5, :] + taps[0:1, :] * buf[5 : 5 + Q, :]
    for k in range(1, 4):
        out = out + taps[k : k + 1, :] * buf[5 + k : 5 + k + Q, :]
    return out


def forward_kernel(first_layer, half, base, inner, scal, *refs):
    it = iter(refs)
    if first_layer:
        mine, theirs = next(it), next(it)
    else:
        hid_prev, mine, theirs = next(it), next(it), next(it)
    gain, w_gate, w_value, w_state, w_step, w_out = (next(it) for _ in range(6))
    taps_v, taps_s, bias, decay_log, skip, gain_in = (next(it) for _ in range(6))
    h_in, vt_in, st_in = (next(it) for _ in range(3))
    if not first_layer:
        hid_out = next(it)
    low_out, gate_out, vin_out, cv_out, y_out, sin_out, cs_out, dt_out, hs_out = (
        next(it) for _ in range(9)
    )
    h_last, vt_last, st_last, keep, send = (next(it) for _ in range(5))
    buf, acc, sq, vbuf, sbuf, b_s, c_s, bt_s, s_s, step_s, cum_s, cumt_s = (
        next(it) for _ in range(12)
    )

    i, g = pl.program_id(0), pl.program_id(1)
    core = scal[0]
    width = low_out.shape[1]

    @pl.when(g == 0)
    def _():
        @pl.when(i == 0)
        def _():
            h_last[...] = h_in[...]
            vt_last[...] = vt_in[...]
            st_last[...] = st_in[...]

        join_halves(buf, mine, theirs, core, half)
        if first_layer:
            token = base + i * Q + lax.broadcasted_iota(jnp.int32, (Q, 1), 0)
            hid = jnp.where(token < scal[1], buf[:, :width], 0.0)
        else:
            total = buf[:, width : width + 1] + buf[:, width + P_SIZE : width + P_SIZE + 1]
            hid = hid_prev[...] + lax.rsqrt(total / inner + EPS) * buf[:, :width]
            hid_out[...] = hid
        low_out[...] = (hid * lax.rsqrt(row_mean(hid * hid) + EPS) * gain[...]).astype(BF16)
        low = low_out[...]
        s_in = nn(low, w_state[...])
        sin_out[...] = s_in.astype(BF16)
        sbuf[0:8, :] = st_last[...]
        sbuf[8 : 8 + Q, :] = s_in
        st_last[...] = s_in[Q - 8 : Q, :]
        cs = conv_rows(sbuf, taps_s)
        cs_out[...] = cs
        states = cs * sigmoid(cs)
        b_val, c_val = states[:, :LANES], states[:, LANES:]
        b_s[...] = b_val.astype(BF16)
        c_s[...] = c_val.astype(BF16)
        bt_s[...] = b_val.T.astype(BF16)
        s_s[...] = nt(c_s[...], b_s[...])
        dt = nn(low, w_step[...])
        dt_out[...] = dt
        step = softplus(dt + bias[...])
        cum = -exact(triangle(True).astype(F32), step * jnp.exp(decay_log[...]))
        step_s[...] = step
        cum_s[...] = cum
        cumt_s[...] = cum.T
        acc[...] = jnp.zeros_like(acc)
        sq[...] = jnp.zeros_like(sq)

    low = low_out[...]
    gate = nn(low, w_gate[...])
    gate_out[...] = gate
    v_in = nn(low, w_value[...])
    vin_out[...] = v_in.astype(BF16)
    vbuf[0:8, :] = vt_last[g]
    vbuf[8 : 8 + Q, :] = v_in
    vt_last[g] = v_in[Q - 8 : Q, :]
    cv = conv_rows(vbuf, taps_v)
    cv_out[...] = cv
    val = cv * sigmoid(cv)
    cum_g = pltpu.roll(cum_s[...], lax.rem(LANES - g * HG, LANES), 1)
    step_g = pltpu.roll(step_s[...], lax.rem(LANES - g * HG, LANES), 1)
    cum_e = spread(cum_g)
    scaled = spread(step_g) * val
    scaled_b = scaled.astype(BF16)
    h_enter = h_last[g]
    hs_out[...] = h_enter
    y = nn(c_s[...], h_enter.astype(BF16)) * jnp.exp(cum_e)
    end = cum_e[Q - 1 : Q, :]
    to_end = (scaled * jnp.exp(end - cum_e)).astype(BF16)
    h_last[g] = h_enter * jnp.exp(end) + nn(bt_s[...], to_end)
    causal = triangle(True)
    tiles = []
    for q in range(GC // LANES):
        tile = jnp.zeros((Q, LANES), F32)
        for parity in range(2):
            j = 2 * q + parity
            gaps = cum_g[:, j : j + 1] - cumt_s[pl.ds(g * HG + j, 1), :]
            weights = jnp.exp(jnp.where(causal, gaps, -1e30))
            mix = (s_s[...] * weights).astype(BF16)
            tile = tile + nn(mix, head_part(scaled_b[:, q * LANES : (q + 1) * LANES], parity))
        tiles.append(tile)
    y = y + jnp.concatenate(tiles, axis=1)
    y_out[...] = y
    gated = (y + skip[...] * val) * (gate * sigmoid(gate))
    sq[...] += jnp.sum(gated * gated, axis=1, keepdims=True)
    acc[:, :width] += nt((gated * gain_in[...]).astype(BF16), w_out[...])

    @pl.when(g == pl.num_programs(1) - 1)
    def _():
        acc[:, width:] = jnp.broadcast_to(sq[:, 0:1], (Q, LANES))
        split_halves(acc, keep, send, core, half)


def backward_kernel(top, bottom, half, base, inner, scal, *refs):
    it = iter(refs)
    if top:
        hid_ref, cot = next(it), next(it)
    else:
        hid_ref, dh_prev, dl_mine, dl_theirs = (next(it) for _ in range(4))
    br_mine, br_theirs, gain = (next(it) for _ in range(3))
    w_gate, w_value, w_state, w_step, w_out = (next(it) for _ in range(5))
    taps_v, taps_s, bias, decay_log, skip, gain_in = (next(it) for _ in range(6))
    gate_ref, vin_ref, cv_ref, y_ref, sin_ref, cs_ref, dt_ref, hs_ref = (next(it) for _ in range(8))
    dh_c, av_c, as_c, ah_c, ag_c = (next(it) for _ in range(5))
    if top:
        result = next(it)
    dh_out, gb_out, go_out, dgate_out, dval_out, dst_out, dstep_out = (next(it) for _ in range(7))
    keep, send = next(it), next(it)
    d_state, acc_v, acc_s, acc_h, acc_g = (next(it) for _ in range(5))
    buf, acc, dst_s, db_s, dc_s, vbuf, sbuf = (next(it) for _ in range(7))
    b_s, c_s, ct_s, st_s, step_s, cum_s, cumt_s, rows_s, dcum_s, dstep_s, end_s = (
        next(it) for _ in range(11)
    )

    i, g = pl.program_id(0), pl.program_id(1)
    core = scal[0]
    width = gb_out.shape[1]

    @pl.when(g == 0)
    def _():
        @pl.when(i == 0)
        def _():
            d_state[...] = dh_c[...]
            acc_v[...] = av_c[...]
            acc_s[...] = as_c[...]
            acc_h[...] = ah_c[...]
            acc_g[...] = ag_c[...]

        if not top:
            join_halves(acc, dl_mine, dl_theirs, core, half)
        join_halves(buf, br_mine, br_theirs, core, half)
        total = buf[:, width : width + 1] + buf[:, width + P_SIZE : width + P_SIZE + 1]
        scale = lax.rsqrt(total / inner + EPS)
        if top:
            hid = hid_ref[...] + scale * buf[:, :width]
        else:
            hid = hid_ref[...]
        r = lax.rsqrt(row_mean(hid * hid) + EPS)
        normed = hid * r
        if top:
            token = base + (pl.num_programs(0) - 1 - i) * Q + lax.broadcasted_iota(jnp.int32, (Q, 1), 0)
            valid = token < scal[1]
            result[...] = jnp.where(valid, normed * gain[...], 0.0).astype(BF16)
            upper = jnp.where(valid, cot[...].astype(F32), 0.0)
        else:
            upper = acc[...]
        acc_g[0:1, :] += col_sum(upper * normed)
        dn = upper * gain[...]
        dh = r * (dn - normed * row_mean(dn * normed))
        if not top:
            dh = dh + dh_prev[...]
        gb = dh.astype(BF16)
        gb_out[...] = gb
        stat = jnp.sum(gb.astype(F32) * buf[:, :width], axis=1, keepdims=True)
        rows_s[:, 0:1] = scale
        rows_s[:, 1:2] = scale * scale * scale * stat / inner
        if bottom:
            acc[...] = dh
            split_halves(acc, dh_out, None, core, half)
        else:
            dh_out[...] = dh

        cs = cs_ref[...]
        states = cs * sigmoid(cs)
        b_val, c_val = states[:, :LANES], states[:, LANES:]
        b_s[...] = b_val.astype(BF16)
        c_s[...] = c_val.astype(BF16)
        ct_s[...] = c_val.T.astype(BF16)
        st_s[...] = nt(b_s[...], c_s[...])
        step = softplus(dt_ref[...] + bias[...])
        cum = -exact(triangle(True).astype(F32), step * jnp.exp(decay_log[...]))
        step_s[...] = step
        cum_s[...] = cum
        cumt_s[...] = cum.T
        acc[...] = jnp.zeros_like(acc)
        dst_s[...] = jnp.zeros_like(dst_s)
        db_s[...] = jnp.zeros_like(db_s)
        dc_s[...] = jnp.zeros_like(dc_s)
        dcum_s[...] = jnp.zeros_like(dcum_s)
        dstep_s[...] = jnp.zeros_like(dstep_s)
        end_s[...] = jnp.zeros_like(end_s)

    scale, coef = rows_s[:, 0:1], rows_s[:, 1:2]
    d_go = nn(gb_out[...], w_out[...])
    cv = cv_ref[...]
    sig_v = sigmoid(cv)
    val = cv * sig_v
    gate = gate_ref[...]
    sig_g = sigmoid(gate)
    silu_g = gate * sig_g
    y = y_ref[...]
    mixed = y + skip[...] * val
    gated = mixed * silu_g
    normed_gate = gated * scale
    acc_v[g, 5:6, :] += col_sum(d_go * normed_gate)
    go_out[...] = (normed_gate * gain_in[...]).astype(BF16)
    d_gated = scale * (d_go * gain_in[...]) - gated * coef
    d_gate = (d_gated * mixed * (sig_g * (1.0 + gate * (1.0 - sig_g)))).astype(BF16)
    dgate_out[...] = d_gate
    d_y = d_gated * silu_g
    acc_v[g, 6:7, :] += col_sum(d_y * val)
    d_y_b = d_y.astype(BF16)
    d_y_r = d_y_b.astype(F32)

    cum_g = pltpu.roll(cum_s[...], lax.rem(LANES - g * HG, LANES), 1)
    step_g = pltpu.roll(step_s[...], lax.rem(LANES - g * HG, LANES), 1)
    cum_e = spread(cum_g)
    step_e = spread(step_g)
    scaled = step_e * val
    scaled_b = scaled.astype(BF16)
    scaled_r = scaled_b.astype(F32)
    causal_t = triangle(False)
    tiles = []
    for q in range(GC // LANES):
        tile = jnp.zeros((Q, LANES), F32)
        x_tile = scaled_b[:, q * LANES : (q + 1) * LANES]
        g_tile = d_y_b[:, q * LANES : (q + 1) * LANES]
        for parity in range(2):
            j = 2 * q + parity
            gaps = cumt_s[pl.ds(g * HG + j, 1), :] - cum_g[:, j : j + 1]
            weights = jnp.exp(jnp.where(causal_t, gaps, -1e30))
            mix = (st_s[...] * weights).astype(BF16)
            part = head_part(g_tile, parity)
            tile = tile + nn(mix, part)
            dst_s[...] += nt(x_tile, part) * weights
        tiles.append(tile)
    d_x = jnp.concatenate(tiles, axis=1)
    end = cum_e[Q - 1 : Q, :]
    exp_end = jnp.exp(end)
    to_end = jnp.exp(end - cum_e)
    h_enter = hs_ref[...]
    d_out = d_state[g]
    d_out_b = d_out.astype(BF16)
    d_across = (d_y * jnp.exp(cum_e)).astype(BF16)
    dc_s[...] += nt(d_across, h_enter.astype(BF16))
    db_s[...] += nt((scaled * to_end).astype(BF16), d_out_b)
    d_x_end = to_end * nn(b_s[...], d_out_b)
    d_state[g] = nn(ct_s[...], d_across) + exp_end * d_out
    end_s[...] = gather_heads(
        end_s[...],
        jnp.broadcast_to(col_sum(scaled_r * d_x_end) + exp_end * col_sum(h_enter * d_out), (8, GC)),
        g,
    )
    d_x = d_x + d_x_end
    dcum_s[...] = gather_heads(dcum_s[...], d_y_r * y - scaled_r * d_x, g)
    dstep_s[...] = gather_heads(dstep_s[...], val * d_x, g)
    d_val = skip[...] * d_y + step_e * d_x
    d_cv = d_val * (sig_v * (1.0 + cv * (1.0 - sig_v)))
    vbuf[0:Q, :] = d_cv
    vbuf[Q : Q + 8, :] = acc_v[g, 8:16, :]
    acc_v[g, 8:16, :] = d_cv[0:8, :]
    v_in = vin_ref[...].astype(F32)
    d_vin = taps_v[3:4, :] * d_cv
    acc_v[g, 3:4, :] += col_sum(v_in * d_cv)
    acc_v[g, 4:5, :] += col_sum(d_cv)
    for k in range(3):
        shifted = vbuf[3 - k : 3 - k + Q, :]
        d_vin = d_vin + taps_v[k : k + 1, :] * shifted
        acc_v[g, k : k + 1, :] += col_sum(v_in * shifted)
    d_vin_b = d_vin.astype(BF16)
    dval_out[...] = d_vin_b
    acc[...] += nt(d_gate, w_gate[...]) + nt(d_vin_b, w_value[...])

    @pl.when(g == pl.num_programs(1) - 1)
    def _():
        decay = jnp.exp(decay_log[...])
        step = step_s[...]
        d_log = exact(triangle(False).astype(F32), dcum_s[...]) + end_s[0:1, :]
        acc_h[1:2, :] += col_sum(d_log * step) * (-decay)
        d_step = (dstep_s[...] - decay * d_log) * sigmoid(dt_ref[...] + bias[...])
        acc_h[0:1, :] += col_sum(d_step)
        d_step_b = d_step.astype(BF16)
        dstep_out[...] = d_step_b
        d_scores = dst_s[...]
        d_b = db_s[...] + nn(d_scores.astype(BF16), c_s[...])
        d_c = dc_s[...] + nn(d_scores.T.astype(BF16), b_s[...])
        cs = cs_ref[...]
        sig_s = sigmoid(cs)
        d_cs = jnp.concatenate([d_b, d_c], axis=1) * (sig_s * (1.0 + cs * (1.0 - sig_s)))
        sbuf[0:Q, :] = d_cs
        sbuf[Q : Q + 8, :] = acc_s[8:16, :]
        acc_s[8:16, :] = d_cs[0:8, :]
        s_in = sin_ref[...].astype(F32)
        d_sin = taps_s[3:4, :] * d_cs
        acc_s[3:4, :] += col_sum(s_in * d_cs)
        acc_s[4:5, :] += col_sum(d_cs)
        for k in range(3):
            shifted = sbuf[3 - k : 3 - k + Q, :]
            d_sin = d_sin + taps_s[k : k + 1, :] * shifted
            acc_s[k : k + 1, :] += col_sum(s_in * shifted)
        d_sin_b = d_sin.astype(BF16)
        dst_out[...] = d_sin_b
        acc[...] += nt(d_sin_b, w_state[...]) + nt(d_step_b, w_step[...])
        split_halves(acc, keep, send, core, half)


def layer_specs(l, width):
    return [
        pl.BlockSpec((None, width, GC), lambda i, g, l=l: (l, 0, g)),
        pl.BlockSpec((None, width, GC), lambda i, g, l=l: (l, 0, g)),
        pl.BlockSpec((None, width, 2 * LANES), lambda i, g, l=l: (l, 0, 0)),
        pl.BlockSpec((None, width, LANES), lambda i, g, l=l: (l, 0, 0)),
        pl.BlockSpec((None, width, GC), lambda i, g, l=l: (l, 0, g)),
        pl.BlockSpec((None, 5, GC), lambda i, g, l=l: (l, 0, g)),
        pl.BlockSpec((None, 5, 2 * LANES), lambda i, g, l=l: (l, 0, 0)),
        pl.BlockSpec((None, 1, LANES), lambda i, g, l=l: (l, 0, 0)),
        pl.BlockSpec((None, 1, LANES), lambda i, g, l=l: (l, 0, 0)),
        pl.BlockSpec((None, 1, GC), lambda i, g, l=l: (l, 0, g)),
        pl.BlockSpec((None, 1, GC), lambda i, g, l=l: (l, 0, g)),
    ]


def whole(shape):
    return pl.BlockSpec(shape, lambda i, g: (0,) * len(shape))


def shape(dims, dtype=F32):
    return jax.ShapeDtypeStruct(dims, dtype)


def forward_call(l, base, half, inner, scal, hid_prev, mine, theirs, gains, weights, carry):
    first = hid_prev is None
    width = weights[0].shape[1]
    groups = weights[0].shape[2] // GC
    cols = groups * GC
    rows = mine.shape[0] * 2
    chunks = rows // Q
    wide = mine.shape[1]

    def block(h, w):
        return pl.BlockSpec((h, w), lambda i, g: (i, 0))

    def grouped(h, w):
        return pl.BlockSpec((h, w), lambda i, g: (i, g))

    in_specs = [pl.BlockSpec(memory_space=pltpu.SMEM)]
    args = [scal]
    if not first:
        in_specs.append(block(Q, width))
        args.append(hid_prev)
    in_specs += [block(Q // 2, wide), block(Q // 2, wide)]
    args += [mine, theirs]
    in_specs.append(pl.BlockSpec((None, 1, width), lambda i, g, l=l: (l, 0, 0)))
    args.append(gains)
    in_specs += layer_specs(l, width)
    args += list(weights)
    carry_shapes = [(groups, LANES, GC), (groups, 8, GC), (8, 2 * LANES)]
    in_specs += [whole(s) for s in carry_shapes]
    args += list(carry)
    out_specs, out_shape = [], []
    if not first:
        out_specs.append(block(Q, width))
        out_shape.append(shape((rows, width)))
    out_specs += [
        block(Q, width),
        grouped(Q, GC),
        grouped(Q, GC),
        grouped(Q, GC),
        grouped(Q, GC),
        block(Q, 2 * LANES),
        block(Q, 2 * LANES),
        block(Q, LANES),
        pl.BlockSpec((None, None, LANES, GC), lambda i, g: (i, g, 0, 0)),
    ]
    out_shape += [
        shape((rows, width), BF16),
        shape((rows, cols)),
        shape((rows, cols), BF16),
        shape((rows, cols)),
        shape((rows, cols)),
        shape((rows, 2 * LANES), BF16),
        shape((rows, 2 * LANES)),
        shape((rows, LANES)),
        shape((chunks, groups, LANES, GC)),
    ]
    out_specs += [whole(s) for s in carry_shapes]
    out_shape += [shape(s) for s in carry_shapes]
    out_specs += [block(Q // 2, width + LANES)] * 2
    out_shape += [shape((rows // 2, width + LANES))] * 2
    scratch = [
        pltpu.VMEM((Q, width + LANES), F32),
        pltpu.VMEM((Q, width + LANES), F32),
        pltpu.VMEM((Q, LANES), F32),
        pltpu.VMEM((Q + 8, GC), F32),
        pltpu.VMEM((Q + 8, 2 * LANES), F32),
        pltpu.VMEM((Q, LANES), BF16),
        pltpu.VMEM((Q, LANES), BF16),
        pltpu.VMEM((LANES, Q), BF16),
        pltpu.VMEM((Q, Q), F32),
        pltpu.VMEM((Q, LANES), F32),
        pltpu.VMEM((Q, LANES), F32),
        pltpu.VMEM((LANES, Q), F32),
    ]
    outs = pl.pallas_call(
        functools.partial(forward_kernel, first, half, base, inner),
        grid=(chunks, groups),
        in_specs=in_specs,
        out_specs=out_specs,
        out_shape=out_shape,
        scratch_shapes=scratch,
        compiler_params=pltpu.CompilerParams(
            dimension_semantics=("arbitrary", "arbitrary"), vmem_limit_bytes=VMEM_LIMIT
        ),
        cost_estimate=pl.CostEstimate(
            flops=rows * 14_000_000, bytes_accessed=20_000_000, transcendentals=rows * 4000
        ),
        name="layer_forward",
    )(*args)
    hid = None
    if not first:
        hid, outs = outs[0], outs[1:]
    return hid, outs[0], tuple(outs[1:9]), tuple(outs[9:12]), outs[12], outs[13]


def backward_call(l, top, bottom, base, half, inner, scal, lead, branch, gains, weights, saved, carry):
    width = weights[0].shape[1]
    groups = weights[0].shape[2] // GC
    cols = groups * GC
    rows = branch[0].shape[0] * 2
    chunks = rows // Q

    def block(h, w):
        return pl.BlockSpec((h, w), lambda i, g: (chunks - 1 - i, 0))

    def grouped(h, w):
        return pl.BlockSpec((h, w), lambda i, g: (chunks - 1 - i, g))

    in_specs = [pl.BlockSpec(memory_space=pltpu.SMEM)]
    if top:
        in_specs += [block(Q, width), block(Q, width)]
    else:
        in_specs += [block(Q, width), block(Q, width), block(Q // 2, width), block(Q // 2, width)]
    in_specs += [block(Q // 2, width + LANES)] * 2
    in_specs.append(pl.BlockSpec((None, 1, width), lambda i, g, l=l: (l + 1, 0, 0)))
    in_specs += layer_specs(l, width)
    in_specs += [
        grouped(Q, GC),
        grouped(Q, GC),
        grouped(Q, GC),
        grouped(Q, GC),
        block(Q, 2 * LANES),
        block(Q, 2 * LANES),
        block(Q, LANES),
        pl.BlockSpec((None, None, LANES, GC), lambda i, g: (chunks - 1 - i, g, 0, 0)),
    ]
    carry_shapes = [(groups, LANES, GC), (groups, 16, GC), (16, 2 * LANES), (8, LANES), (8, width)]
    in_specs += [whole(s) for s in carry_shapes]
    out_specs, out_shape = [], []
    if top:
        out_specs.append(block(Q, width))
        out_shape.append(shape((rows, width), BF16))
    dh_rows = Q // 2 if bottom else Q
    out_specs += [
        block(dh_rows, width),
        block(Q, width),
        grouped(Q, GC),
        grouped(Q, GC),
        grouped(Q, GC),
        block(Q, 2 * LANES),
        block(Q, LANES),
        block(Q // 2, width),
        block(Q // 2, width),
    ]
    out_shape += [
        shape((chunks * dh_rows, width)),
        shape((rows, width), BF16),
        shape((rows, cols), BF16),
        shape((rows, cols), BF16),
        shape((rows, cols), BF16),
        shape((rows, 2 * LANES), BF16),
        shape((rows, LANES), BF16),
        shape((rows // 2, width)),
        shape((rows // 2, width)),
    ]
    out_specs += [whole(s) for s in carry_shapes]
    out_shape += [shape(s) for s in carry_shapes]
    scratch = [
        pltpu.VMEM((Q, width + LANES), F32),
        pltpu.VMEM((Q, width), F32),
        pltpu.VMEM((Q, Q), F32),
        pltpu.VMEM((Q, LANES), F32),
        pltpu.VMEM((Q, LANES), F32),
        pltpu.VMEM((Q + 8, GC), F32),
        pltpu.VMEM((Q + 8, 2 * LANES), F32),
        pltpu.VMEM((Q, LANES), BF16),
        pltpu.VMEM((Q, LANES), BF16),
        pltpu.VMEM((LANES, Q), BF16),
        pltpu.VMEM((Q, Q), F32),
        pltpu.VMEM((Q, LANES), F32),
        pltpu.VMEM((Q, LANES), F32),
        pltpu.VMEM((LANES, Q), F32),
        pltpu.VMEM((Q, LANES), F32),
        pltpu.VMEM((Q, LANES), F32),
        pltpu.VMEM((Q, LANES), F32),
        pltpu.VMEM((8, LANES), F32),
    ]
    outs = pl.pallas_call(
        functools.partial(backward_kernel, top, bottom, half, base, inner),
        grid=(chunks, groups),
        in_specs=in_specs,
        out_specs=out_specs,
        out_shape=out_shape,
        scratch_shapes=scratch,
        compiler_params=pltpu.CompilerParams(
            dimension_semantics=("arbitrary", "arbitrary"), vmem_limit_bytes=VMEM_LIMIT
        ),
        cost_estimate=pl.CostEstimate(
            flops=rows * 20_000_000, bytes_accessed=25_000_000, transcendentals=rows * 4000
        ),
        name="layer_backward",
    )(scal, *lead, *branch, gains, *weights, *saved, *carry)
    result = None
    if top:
        result, outs = outs[0], outs[1:]
    dh, gb, go, dgate, dval, dst, dstep, keep, send = outs[:9]
    return result, dh, gb, go, (dgate, dval, dst, dstep), keep, send, tuple(outs[9:])


def pairs(axis, bit):
    return [(i, i ^ bit) for i in range(lax.axis_size(axis))]


def sum_pairs(value, axis, bit):
    return value + lax.ppermute(value, axis, pairs(axis, bit))


def two_terms(wide, width):
    main = wide[:, :width].astype(BF16)
    if wide.shape[1] == width:
        return main
    tail = wide[:, width:]
    lead = lax.reduce_precision(tail, 8, 7)
    lane = lax.broadcasted_iota(jnp.int32, tail.shape, 1)
    tail = jnp.where(lane < P_SIZE, lead, tail - lead).astype(BF16)
    return jnp.concatenate([main, tail], axis=1)


def sum_tensor_half(keep, send, width):
    chip = keep + lax.ppermute(send, "tensor", pairs("tensor", 1))
    own = lax.optimization_barrier(two_terms(chip, width))
    other = lax.ppermute(own, "tensor", pairs("tensor", 2))
    return own.astype(F32) + other.astype(F32)


def both_halves(half_rows):
    return half_rows, lax.ppermute(half_rows, "tensor", pairs("tensor", 1))


def pad_lanes(v):
    return jnp.pad(v, [(0, 0)] * (v.ndim - 1) + [(0, LANES - v.shape[-1])])


def per_device(
    x_in,
    cotangent,
    lengths,
    deal_order,
    norm_gains,
    proj_gate,
    proj_value,
    proj_state,
    proj_step,
    proj_out,
    conv_value,
    conv_state,
    step_bias,
    decay_log,
    skip_gain,
    inner_gain,
):
    _, slot_len, width = cotangent.shape
    layers = proj_gate.shape[0]
    cols = proj_gate.shape[2]
    heads = step_bias.shape[1]
    inner = cols * lax.axis_size("tensor")
    dp = lax.axis_size("dp")
    groups = cols // GC
    half = x_in.shape[1] // 2
    me = lax.axis_index("dp")
    core = lax.rem(lax.axis_index("tensor"), 2)
    length = jnp.take(lengths, lax.dynamic_index_in_dim(deal_order, me, keepdims=False))
    scal = jnp.stack([core, length]).astype(jnp.int32)

    x_half = lax.dynamic_slice_in_dim(x_in, core * half, half, axis=1)
    x_dealt = jnp.take(x_half, deal_order, axis=0)
    x_mine = lax.all_to_all(x_dealt, "dp", split_axis=0, concat_axis=0, tiled=True)
    x_mine = x_mine.reshape(slot_len // 2, width)
    x_mine, x_theirs = both_halves(x_mine)

    gains = norm_gains[:, None, :]
    weights = (
        proj_gate,
        proj_value,
        proj_state,
        pad_lanes(proj_step),
        proj_out,
        conv_value,
        conv_state,
        pad_lanes(step_bias)[:, None, :],
        pad_lanes(decay_log)[:, None, :],
        jnp.repeat(skip_gain, P_SIZE, axis=1)[:, None, :],
        inner_gain[:, None, :],
    )
    cot = cotangent.reshape(slot_len, width)

    rows_f = CHUNKS_F * Q
    calls_f = slot_len // rows_f
    hids, lows, saves, branches = [], [], [], []
    lead = [
        (None, x_mine[c * rows_f // 2 : (c + 1) * rows_f // 2], x_theirs[c * rows_f // 2 : (c + 1) * rows_f // 2])
        for c in range(calls_f)
    ]
    for l in range(layers):
        carry = (
            jnp.zeros((groups, LANES, GC), F32),
            jnp.zeros((groups, 8, GC), F32),
            jnp.zeros((8, 2 * LANES), F32),
        )
        hid_l, low_l, save_l, branch_l = [], [], [], []
        for c in range(calls_f):
            hid, low, saved, carry, keep, send = forward_call(
                l, c * rows_f, half, inner, scal, *lead[c], gains, weights, carry
            )
            hid_l.append(hid)
            low_l.append(low)
            save_l.append(saved)
            branch_l.append(both_halves(sum_tensor_half(keep, send, width)))
        hids.append(hid_l)
        lows.append(low_l)
        saves.append(save_l)
        branches.append(branch_l)
        if l == 0:
            lead = []
            for c in range(calls_f):
                token = c * rows_f + lax.broadcasted_iota(jnp.int32, (rows_f, 1), 0)
                x_rows = join_rows(x_mine, x_theirs, core, half, c * rows_f // 2, rows_f // 2)
                hid_l[c] = jnp.where(token < length, x_rows.astype(F32), 0.0)
        lead = [(hid_l[c], *branch_l[c]) for c in range(calls_f)]

    results = [None] * calls_f
    d_hids = [None] * calls_f
    d_lows = [None] * calls_f
    gain_grads, v_grads, s_grads, h_grads, scattered = [], [], [], [], []
    for l in reversed(range(layers)):
        top, bottom = l == layers - 1, l == 0
        carry = (
            jnp.zeros((groups, LANES, GC), F32),
            jnp.zeros((groups, 16, GC), F32),
            jnp.zeros((16, 2 * LANES), F32),
            jnp.zeros((8, LANES), F32),
            jnp.zeros((8, width), F32),
        )
        gbs, gos, ds = [None] * calls_f, [None] * calls_f, [None] * calls_f
        new_d_hids, new_d_lows = [None] * calls_f, [None] * calls_f
        for c in reversed(range(calls_f)):
            base = c * rows_f
            if top:
                first = (hids[l][c], cot[base : base + rows_f])
            else:
                first = (hids[l + 1][c], d_hids[c], *d_lows[c])
            result, dh, gb, go, d_in, keep, send, carry = backward_call(
                l, top, bottom, base, half, inner, scal, first, branches[l][c], gains, weights, saves[l][c], carry
            )
            if top:
                results[c] = result
            gbs[c], gos[c], ds[c] = gb, go, d_in
            new_d_hids[c] = dh
            summed = sum_tensor_half(keep, send, width)
            new_d_lows[c] = summed if bottom else both_halves(summed)
        d_hids, d_lows = new_d_hids, new_d_lows
        _, acc_v, acc_s, acc_h, acc_g = carry
        gain_grads.insert(0, acc_g[0])
        v_grads.insert(0, acc_v)
        s_grads.insert(0, acc_s[:5])
        h_grads.insert(0, acc_h[:2])
        low = jnp.concatenate(lows[l], axis=0)
        d_all = jnp.concatenate([jnp.concatenate(parts, axis=1) for parts in ds], axis=0)
        g_in = tn(low, d_all).astype(BF16)
        g_out = tn(jnp.concatenate(gbs, axis=0), jnp.concatenate(gos, axis=0)).astype(BF16)
        pieces = [g_out, g_in]
        scattered.insert(
            0, [lax.psum_scatter(p, "dp", scatter_dimension=0, tiled=True) for p in pieces]
        )

    d_low = jnp.concatenate(d_lows, axis=0)
    d_hid = jnp.concatenate(d_hids, axis=0)
    token = (
        lax.broadcasted_iota(jnp.int32, (dp, half, 1), 0) * (2 * half)
        + lax.broadcasted_iota(jnp.int32, (dp, half, 1), 1)
        + core * half
    ).reshape(slot_len // 2, 1)
    valid = (token < length).astype(F32)
    hid = x_mine.astype(F32) * valid
    r = lax.rsqrt(row_mean(hid * hid) + EPS)
    normed = hid * r
    gain_first = jnp.sum(d_low * normed, axis=0)
    dn = d_low * norm_gains[0]
    d_hid = d_hid + r * (dn - normed * row_mean(dn * normed))
    grad_in = (d_hid * valid).astype(BF16).reshape(dp, half, width)
    returned = lax.all_to_all(grad_in, "dp", split_axis=0, concat_axis=0, tiled=True)
    mine, theirs = both_halves(returned)
    grad_x = jnp.where(
        core == 0, jnp.concatenate([mine, theirs], axis=1), jnp.concatenate([theirs, mine], axis=1)
    )
    inverse = jnp.sum(
        jnp.where(deal_order[None, :] == jnp.arange(dp)[:, None], jnp.arange(dp)[None, :], 0), axis=1
    )
    grad_x = jnp.take(grad_x, inverse, axis=0)

    v_all = jnp.stack(v_grads)
    v_all = jnp.swapaxes(v_all, 1, 2).reshape(layers, 16, cols)
    s_all = jnp.stack(s_grads)
    h_all = jnp.stack(h_grads)
    gain_first = sum_pairs(gain_first, "tensor", 1)
    gain_all = jnp.stack([gain_first] + gain_grads)
    for bit in (1, 2):
        s_all = sum_pairs(s_all, "tensor", bit)
    small = jnp.concatenate(
        [v_all[:, :7].reshape(-1), s_all.reshape(-1), h_all.reshape(-1), gain_all.reshape(-1)]
    )
    small = small.reshape(-1, LANES)
    bit = 1
    while bit < dp:
        small = sum_pairs(small, "dp", bit)
        bit *= 2
    small = small.reshape(-1)
    n_v, n_s, n_h = layers * 7 * cols, s_all.size, h_all.size
    v_sum = small[:n_v].reshape(layers, 7, cols)
    s_sum = small[n_v : n_v + n_s].reshape(s_all.shape)
    h_sum = small[n_v + n_s : n_v + n_s + n_h].reshape(h_all.shape)
    gain_sum = small[n_v + n_s + n_h :].reshape(gain_all.shape)
    piece = width // dp
    gain_own = lax.dynamic_slice_in_dim(gain_sum, me * piece, piece, axis=1)

    g_out = jnp.stack([s[0] for s in scattered]).astype(F32)
    g_in = jnp.stack([s[1] for s in scattered]).astype(F32)
    g_gate, g_value = g_in[:, :, :cols], g_in[:, :, cols : 2 * cols]
    g_state = g_in[:, :, 2 * cols : 2 * cols + 2 * LANES]
    for bit in (1, 2):
        g_state = sum_pairs(g_state, "tensor", bit)
    g_step = g_in[:, :, 2 * cols + 2 * LANES :][:, :, :heads]
    skip_grad = v_sum[:, 6].reshape(layers, heads, P_SIZE).sum(axis=2)
    return (
        jnp.concatenate(results, axis=0)[None],
        grad_x,
        gain_own,
        g_gate,
        g_value,
        g_state,
        g_step,
        g_out,
        v_sum[:, :5],
        s_sum,
        h_sum[:, 0, :heads],
        h_sum[:, 1, :heads],
        skip_grad,
        v_sum[:, 5],
    )


def join_rows(mine, theirs, core, half, start, count):
    own = mine[start : start + count].reshape(-1, half, mine.shape[1])
    other = theirs[start : start + count].reshape(-1, half, mine.shape[1])
    first = jnp.where(core == 0, own, other)
    second = jnp.where(core == 0, other, own)
    return jnp.concatenate([first, second], axis=1).reshape(2 * count, mine.shape[1])


def solution(mesh):
    return jax.shard_map(
        per_device,
        mesh=mesh,
        in_specs=(
            P(None, "dp", None),
            P("dp", None, None),
            P(),
            P(),
            P(),
            P(None, None, "tensor"),
            P(None, None, "tensor"),
            P(),
            P(None, None, "tensor"),
            P(None, None, "tensor"),
            P(None, None, "tensor"),
            P(),
            P(None, "tensor"),
            P(None, "tensor"),
            P(None, "tensor"),
            P(None, "tensor"),
        ),
        out_specs=(
            P("dp", None, None),
            P(None, "dp", None),
            P(None, "dp"),
            P(None, "dp", "tensor"),
            P(None, "dp", "tensor"),
            P(None, "dp", None),
            P(None, "dp", "tensor"),
            P(None, "dp", "tensor"),
            P(None, None, "tensor"),
            P(),
            P(None, "tensor"),
            P(None, "tensor"),
            P(None, "tensor"),
            P(None, "tensor"),
        ),
        check_vma=False,
    )
```

```python
import functools

import jax
import jax.numpy as jnp
from jax import lax
from jax.experimental import pallas as pl
from jax.experimental.pallas import tpu as pltpu
from jax.sharding import PartitionSpec as P

P_SIZE = 64
Q = 256
GC = 256
HG = GC // P_SIZE
LANES = 128
EPS = 1e-05
CHUNKS = 1
VMEM_LIMIT = 56 * 1024 * 1024

F32 = jnp.float32
BF16 = jnp.bfloat16


def nn(a, b):
    return jnp.dot(a, b, preferred_element_type=F32)


def nt(a, b):
    return lax.dot_general(a, b, (((1,), (1,)), ((), ())), preferred_element_type=F32)


def tn(a, b):
    return lax.dot_general(a, b, (((0,), (0,)), ((), ())), preferred_element_type=F32)


def exact(a, b):
    return jnp.dot(a, b, preferred_element_type=F32, precision=lax.Precision.HIGHEST)


def sigmoid(v):
    return 1.0 / (1.0 + jnp.exp(-v))


def softplus(v):
    return jnp.maximum(v, 0.0) + jnp.log1p(jnp.exp(-jnp.abs(v)))


def triangle(lower):
    rows = lax.broadcasted_iota(jnp.int32, (Q, Q), 0)
    cols = lax.broadcasted_iota(jnp.int32, (Q, Q), 1)
    return rows >= cols if lower else cols >= rows


def row_mean(v):
    return jnp.mean(v, axis=1, keepdims=True)


def col_sum(v):
    return jnp.sum(v, axis=0, keepdims=True)


def join_halves(dst, mine, theirs, core, half):
    width = mine[0].shape[-1]
    for m in range(Q // (2 * half)):
        rows = slice(half * m, half * m + half)
        for terms, side in ((mine, core), (theirs, 1 - core)):
            total = terms[0][rows, :].astype(F32)
            for term in terms[1:]:
                total = total + term[rows, :].astype(F32)
            dst[pl.ds(pl.multiple_of(2 * half * m + half * side, 8), half), :width] = total


def split_halves(src, keep, send, core, half):
    width = keep.shape[-1]
    for m in range(Q // (2 * half)):
        own = pl.multiple_of(2 * half * m + half * core, 8)
        keep[half * m : half * m + half, :] = src[pl.ds(own, half), :width].astype(keep.dtype)
        if send is not None:
            other = pl.multiple_of(2 * half * m + half * (1 - core), 8)
            send[half * m : half * m + half, :] = src[pl.ds(other, half), :width].astype(send.dtype)


def spread(per_head):
    rows = per_head.shape[0]
    lane = lax.broadcasted_iota(jnp.int32, (rows, LANES), 1)
    tiles = []
    for q in range(GC // LANES):
        left = jnp.broadcast_to(per_head[:, 2 * q : 2 * q + 1], (rows, LANES))
        right = jnp.broadcast_to(per_head[:, 2 * q + 1 : 2 * q + 2], (rows, LANES))
        tiles.append(jnp.where(lane < P_SIZE, left, right))
    return jnp.concatenate(tiles, axis=1)


def to_group(per_head, group):
    return pltpu.roll(per_head, lax.rem(LANES - group * HG, LANES), 1)


def skip_row(heads_p, group):
    return spread(to_group(jnp.broadcast_to(heads_p[2:3, :], (8, LANES)), group))[0:1, :]


def head_part(tile, parity):
    lane = lax.broadcasted_iota(jnp.int32, tile.shape, 1)
    return jnp.where((lane < P_SIZE) == (parity == 0), tile, jnp.zeros_like(tile))


def gather_heads(acc, cols, group):
    lane = lax.broadcasted_iota(jnp.int32, (cols.shape[0], LANES), 1)
    for j in range(HG):
        tile = head_part(cols[:, (j // 2) * LANES : (j // 2 + 1) * LANES], j % 2)
        total = jnp.sum(tile, axis=1, keepdims=True)
        acc = acc + jnp.where(lane == group * HG + j, total, 0.0)
    return acc


def conv_rows(buf, taps):
    out = taps[4:5, :] + taps[0:1, :] * buf[5 : 5 + Q, :]
    for k in range(1, 4):
        out = out + taps[k : k + 1, :] * buf[5 + k : 5 + k + Q, :]
    return out


def forward_kernel(first_layer, fresh, n_skip, l, half, base, inner, scal, *refs):
    it = iter(refs)
    if not first_layer:
        hid_prev = next(it)
    count = 1 if first_layer else 2
    mine = [next(it) for _ in range(count)]
    theirs = [next(it) for _ in range(count)]
    gains = next(it)
    w_gate, w_value, w_state, w_step, w_out = (next(it) for _ in range(5))
    taps_v, taps_s, heads_p, gain_in = (next(it) for _ in range(4))
    if not fresh:
        h_in, vt_in, st_in = (next(it) for _ in range(3))
    for _ in range(n_skip):
        next(it)
    hid_out, low_out, u_out = next(it), next(it), next(it)
    gate_out, vin_out, cv_out, y_out, sin_out, cs_out, dt_out, hs_out = (next(it) for _ in range(8))
    h_last, vt_last, st_last, keep, send = (next(it) for _ in range(5))
    buf, acc, sq, vbuf, sbuf, b_s, c_s, bt_s, s_s, step_s, cum_s, cumt_s = (
        next(it) for _ in range(12)
    )
    gain = gains[l : l + 1, :]
    bias, decay_log = heads_p[0:1, :], heads_p[1:2, :]

    i, g = pl.program_id(0), pl.program_id(1)
    core = scal[0]
    width = low_out.shape[1]

    @pl.when(g == 0)
    def _():
        @pl.when(i == 0)
        def _():
            if fresh:
                h_last[...] = jnp.zeros_like(h_last)
                vt_last[...] = jnp.zeros_like(vt_last)
                st_last[...] = jnp.zeros_like(st_last)
            else:
                h_last[...] = h_in[...]
                vt_last[...] = vt_in[...]
                st_last[...] = st_in[...]

        join_halves(buf, mine, theirs, core, half)
        if first_layer:
            token = base + i * Q + lax.broadcasted_iota(jnp.int32, (Q, 1), 0)
            hid = jnp.where(token < scal[1], buf[:, :width], 0.0)
        else:
            total = buf[:, width : width + 1] + buf[:, width + P_SIZE : width + P_SIZE + 1]
            hid = hid_prev[...] + lax.rsqrt(total / inner + EPS) * buf[:, :width]
        hid_out[...] = hid
        low_out[...] = (hid * lax.rsqrt(row_mean(hid * hid) + EPS) * gain).astype(BF16)
        low = low_out[...]
        s_in = nn(low, w_state[...])
        sin_out[...] = s_in.astype(BF16)
        sbuf[0:8, :] = st_last[...]
        sbuf[8 : 8 + Q, :] = s_in
        st_last[...] = s_in[Q - 8 : Q, :]
        cs = conv_rows(sbuf, taps_s)
        cs_out[...] = cs
        states = cs * sigmoid(cs)
        b_val, c_val = states[:, :LANES], states[:, LANES:]
        b_s[...] = b_val.astype(BF16)
        c_s[...] = c_val.astype(BF16)
        bt_s[...] = b_val.T.astype(BF16)
        s_s[...] = nt(c_s[...], b_s[...])
        dt = nn(low, w_step[...])
        dt_out[...] = dt
        step = softplus(dt + bias)
        cum = -exact(triangle(True).astype(F32), step * jnp.exp(decay_log))
        step_s[...] = step
        cum_s[...] = cum
        cumt_s[...] = cum.T
        acc[...] = jnp.zeros_like(acc)
        sq[...] = jnp.zeros_like(sq)

    low = low_out[...]
    gate = nn(low, w_gate[...])
    gate_out[...] = gate
    v_in = nn(low, w_value[...])
    vin_out[...] = v_in.astype(BF16)
    vbuf[0:8, :] = vt_last[g]
    vbuf[8 : 8 + Q, :] = v_in
    vt_last[g] = v_in[Q - 8 : Q, :]
    cv = conv_rows(vbuf, taps_v)
    cv_out[...] = cv
    val = cv * sigmoid(cv)
    cum_g = to_group(cum_s[...], g)
    step_g = to_group(step_s[...], g)
    cum_e = spread(cum_g)
    scaled = spread(step_g) * val
    scaled_b = scaled.astype(BF16)
    h_enter = h_last[g]
    hs_out[...] = h_enter
    y = nn(c_s[...], h_enter.astype(BF16)) * jnp.exp(cum_e)
    end = cum_e[Q - 1 : Q, :]
    to_end = (scaled * jnp.exp(end - cum_e)).astype(BF16)
    h_last[g] = h_enter * jnp.exp(end) + nn(bt_s[...], to_end)
    causal = triangle(True)
    tiles = []
    for q in range(GC // LANES):
        tile = jnp.zeros((Q, LANES), F32)
        for parity in range(2):
            j = 2 * q + parity
            gaps = cum_g[:, j : j + 1] - cumt_s[pl.ds(g * HG + j, 1), :]
            weights = jnp.exp(jnp.where(causal, gaps, -1e30))
            mix = (s_s[...] * weights).astype(BF16)
            tile = tile + nn(mix, head_part(scaled_b[:, q * LANES : (q + 1) * LANES], parity))
        tiles.append(tile)
    y = y + jnp.concatenate(tiles, axis=1)
    y_out[...] = y
    gated = (y + skip_row(heads_p, g) * val) * (gate * sigmoid(gate))
    sq[...] += jnp.sum(gated * gated, axis=1, keepdims=True)
    u_out[...] = (gated * gain_in[...]).astype(BF16)
    acc[:, :width] += nt(u_out[...], w_out[...])

    @pl.when(g == pl.num_programs(1) - 1)
    def _():
        acc[:, width:] = jnp.broadcast_to(sq[:, 0:1], (Q, LANES))
        split_halves(acc, keep, send, core, half)


def norm_kernel(top, bottom, fresh, n_skip, l, half, base, inner, scal, *refs):
    it = iter(refs)
    hid_ref = next(it)
    if top:
        cot = next(it)
    else:
        dh_prev = next(it)
        dl_mine, dl_theirs = ([next(it), next(it)] for _ in range(2))
    br_mine, br_theirs = ([next(it), next(it)] for _ in range(2))
    gains = next(it)
    if not fresh:
        gain_c = next(it)
    for _ in range(n_skip):
        next(it)
    if top:
        result = next(it)
    dh_out, gb_out, gbs_out, rows_out, gain_acc, buf, low = (next(it) for _ in range(7))
    core = scal[0]
    width = gb_out.shape[1]
    gain = gains[l + 1 : l + 2, :]

    @pl.when(pl.program_id(0) == 0)
    def _():
        gain_acc[...] = jnp.zeros_like(gain_acc) if fresh else gain_c[...]

    join_halves(buf, br_mine, br_theirs, core, half)
    total = buf[:, width : width + 1] + buf[:, width + P_SIZE : width + P_SIZE + 1]
    scale = lax.rsqrt(total / inner + EPS)
    hid = hid_ref[...]
    if top:
        hid = hid + scale * buf[:, :width]
    r = lax.rsqrt(row_mean(hid * hid) + EPS)
    normed = hid * r
    if top:
        token = base + pl.program_id(0) * Q + lax.broadcasted_iota(jnp.int32, (Q, 1), 0)
        valid = token < scal[1]
        result[...] = jnp.where(valid, normed * gain, 0.0).astype(BF16)
        upper = jnp.where(valid, cot[...].astype(F32), 0.0)
    else:
        join_halves(low, dl_mine, dl_theirs, core, half)
        upper = low[...]
    gain_acc[0:1, :] += col_sum(upper * normed)
    dn = upper * gain
    dh = r * (dn - normed * row_mean(dn * normed))
    if not top:
        dh = dh + dh_prev[...]
    gb = dh.astype(BF16)
    gb_out[...] = gb
    gbs_out[...] = (dh * scale).astype(BF16)
    stat = jnp.sum(gb.astype(F32) * buf[:, :width], axis=1, keepdims=True)
    lane = lax.broadcasted_iota(jnp.int32, (Q, LANES), 1)
    rows_out[...] = jnp.where(lane == 0, scale, scale * scale * scale * stat / inner)
    if bottom:
        low[...] = dh
        split_halves(low, dh_out, None, core, half)
    else:
        dh_out[...] = dh


def backward_kernel(fresh, n_skip, l, half, scal, *refs):
    it = iter(refs)
    gb_ref, rows_ref = next(it), next(it)
    w_gate, w_value, w_state, w_step, w_out = (next(it) for _ in range(5))
    taps_v, taps_s, heads_p, gain_in = (next(it) for _ in range(4))
    gate_ref, vin_ref, cv_ref, y_ref, sin_ref, cs_ref, dt_ref, hs_ref = (next(it) for _ in range(8))
    if not fresh:
        dh_c, av_c, as_c, ah_c = (next(it) for _ in range(4))
    for _ in range(n_skip):
        next(it)
    dgate_out, dval_out, dst_out, dstep_out = (next(it) for _ in range(4))
    keep, send = next(it), next(it)
    d_state, acc_v, acc_s, acc_h = (next(it) for _ in range(4))
    acc, dst_s, db_s, dc_s, vbuf, sbuf = (next(it) for _ in range(6))
    b_s, c_s, ct_s, st_s, step_s, cum_s, cumt_s, dcum_s, dstep_s, end_s = (
        next(it) for _ in range(10)
    )

    i, g = pl.program_id(0), pl.program_id(1)
    core = scal[0]
    bias, decay_log = heads_p[0:1, :], heads_p[1:2, :]

    @pl.when(g == 0)
    def _():
        @pl.when(i == 0)
        def _():
            if fresh:
                d_state[...] = jnp.zeros_like(d_state)
                acc_v[...] = jnp.zeros_like(acc_v)
                acc_s[...] = jnp.zeros_like(acc_s)
                acc_h[...] = jnp.zeros_like(acc_h)
            else:
                d_state[...] = dh_c[...]
                acc_v[...] = av_c[...]
                acc_s[...] = as_c[...]
                acc_h[...] = ah_c[...]

        cs = cs_ref[...]
        states = cs * sigmoid(cs)
        b_val, c_val = states[:, :LANES], states[:, LANES:]
        b_s[...] = b_val.astype(BF16)
        c_s[...] = c_val.astype(BF16)
        ct_s[...] = c_val.T.astype(BF16)
        st_s[...] = nt(b_s[...], c_s[...])
        step = softplus(dt_ref[...] + bias)
        cum = -exact(triangle(True).astype(F32), step * jnp.exp(decay_log))
        step_s[...] = step
        cum_s[...] = cum
        cumt_s[...] = cum.T
        acc[...] = jnp.zeros_like(acc)
        dst_s[...] = jnp.zeros_like(dst_s)
        db_s[...] = jnp.zeros_like(db_s)
        dc_s[...] = jnp.zeros_like(dc_s)
        dcum_s[...] = jnp.zeros_like(dcum_s)
        dstep_s[...] = jnp.zeros_like(dstep_s)
        end_s[...] = jnp.zeros_like(end_s)

    scale, coef = rows_ref[:, 0:1], rows_ref[:, 1:2]
    skip = skip_row(heads_p, g)
    d_go = nn(gb_ref[...], w_out[...])
    cv = cv_ref[...]
    sig_v = sigmoid(cv)
    val = cv * sig_v
    gate = gate_ref[...]
    sig_g = sigmoid(gate)
    silu_g = gate * sig_g
    y = y_ref[...]
    mixed = y + skip * val
    gated = mixed * silu_g
    normed_gate = gated * scale
    acc_v[g, 5:6, :] += col_sum(d_go * normed_gate)
    d_gated = scale * (d_go * gain_in[...]) - gated * coef
    d_gate = (d_gated * mixed * (sig_g * (1.0 + gate * (1.0 - sig_g)))).astype(BF16)
    dgate_out[...] = d_gate
    d_y = d_gated * silu_g
    acc_v[g, 6:7, :] += col_sum(d_y * val)
    d_y_b = d_y.astype(BF16)
    d_y_r = d_y_b.astype(F32)

    cum_g = to_group(cum_s[...], g)
    step_g = to_group(step_s[...], g)
    cum_e = spread(cum_g)
    step_e = spread(step_g)
    scaled = step_e * val
    scaled_b = scaled.astype(BF16)
    scaled_r = scaled_b.astype(F32)
    causal_t = triangle(False)
    tiles = []
    for q in range(GC // LANES):
        tile = jnp.zeros((Q, LANES), F32)
        x_tile = scaled_b[:, q * LANES : (q + 1) * LANES]
        g_tile = d_y_b[:, q * LANES : (q + 1) * LANES]
        for parity in range(2):
            j = 2 * q + parity
            gaps = cumt_s[pl.ds(g * HG + j, 1), :] - cum_g[:, j : j + 1]
            weights = jnp.exp(jnp.where(causal_t, gaps, -1e30))
            mix = (st_s[...] * weights).astype(BF16)
            part = head_part(g_tile, parity)
            tile = tile + nn(mix, part)
            dst_s[...] += nt(x_tile, part) * weights
        tiles.append(tile)
    d_x = jnp.concatenate(tiles, axis=1)
    end = cum_e[Q - 1 : Q, :]
    exp_end = jnp.exp(end)
    to_end = jnp.exp(end - cum_e)
    h_enter = hs_ref[...]
    d_out = d_state[g]
    d_out_b = d_out.astype(BF16)
    d_across = (d_y * jnp.exp(cum_e)).astype(BF16)
    dc_s[...] += nt(d_across, h_enter.astype(BF16))
    db_s[...] += nt((scaled * to_end).astype(BF16), d_out_b)
    d_x_end = to_end * nn(b_s[...], d_out_b)
    d_state[g] = nn(ct_s[...], d_across) + exp_end * d_out
    end_s[...] = gather_heads(
        end_s[...],
        jnp.broadcast_to(col_sum(scaled_r * d_x_end) + exp_end * col_sum(h_enter * d_out), (8, GC)),
        g,
    )
    d_x = d_x + d_x_end
    dcum_s[...] = gather_heads(dcum_s[...], d_y_r * y - scaled_r * d_x, g)
    dstep_s[...] = gather_heads(dstep_s[...], val * d_x, g)
    d_val = skip * d_y + step_e * d_x
    d_cv = d_val * (sig_v * (1.0 + cv * (1.0 - sig_v)))
    vbuf[0:Q, :] = d_cv
    vbuf[Q : Q + 8, :] = acc_v[g, 8:16, :]
    acc_v[g, 8:16, :] = d_cv[0:8, :]
    v_in = vin_ref[...].astype(F32)
    d_vin = taps_v[3:4, :] * d_cv
    acc_v[g, 3:4, :] += col_sum(v_in * d_cv)
    acc_v[g, 4:5, :] += col_sum(d_cv)
    for k in range(3):
        shifted = vbuf[3 - k : 3 - k + Q, :]
        d_vin = d_vin + taps_v[k : k + 1, :] * shifted
        acc_v[g, k : k + 1, :] += col_sum(v_in * shifted)
    d_vin_b = d_vin.astype(BF16)
    dval_out[...] = d_vin_b
    acc[...] += nt(d_gate, w_gate[...]) + nt(d_vin_b, w_value[...])

    @pl.when(g == pl.num_programs(1) - 1)
    def _():
        decay = jnp.exp(decay_log)
        step = step_s[...]
        d_log = exact(triangle(False).astype(F32), dcum_s[...]) + end_s[0:1, :]
        acc_h[1:2, :] += col_sum(d_log * step) * (-decay)
        d_step = (dstep_s[...] - decay * d_log) * sigmoid(dt_ref[...] + bias)
        acc_h[0:1, :] += col_sum(d_step)
        d_step_b = d_step.astype(BF16)
        dstep_out[...] = d_step_b
        d_scores = dst_s[...]
        d_b = db_s[...] + nn(d_scores.astype(BF16), c_s[...])
        d_c = dc_s[...] + nn(d_scores.T.astype(BF16), b_s[...])
        cs = cs_ref[...]
        sig_s = sigmoid(cs)
        d_cs = jnp.concatenate([d_b, d_c], axis=1) * (sig_s * (1.0 + cs * (1.0 - sig_s)))
        sbuf[0:Q, :] = d_cs
        sbuf[Q : Q + 8, :] = acc_s[8:16, :]
        acc_s[8:16, :] = d_cs[0:8, :]
        s_in = sin_ref[...].astype(F32)
        d_sin = taps_s[3:4, :] * d_cs
        acc_s[3:4, :] += col_sum(s_in * d_cs)
        acc_s[4:5, :] += col_sum(d_cs)
        for k in range(3):
            shifted = sbuf[3 - k : 3 - k + Q, :]
            d_sin = d_sin + taps_s[k : k + 1, :] * shifted
            acc_s[k : k + 1, :] += col_sum(s_in * shifted)
        d_sin_b = d_sin.astype(BF16)
        dst_out[...] = d_sin_b
        acc[...] += nt(d_sin_b, w_state[...]) + nt(d_step_b, w_step[...])
        split_halves(acc, keep, send, core, half)


def weight_kernel(half, bit, pieces, scal, a_ref, *refs):
    ds = refs[:pieces]
    at = 0
    if bit is None:
        out = refs[-1]
        for d in ds:
            out[:, at : at + d.shape[1]] = tn(a_ref[...], d[...]).astype(BF16)
            at += d.shape[1]
        return
    keep, send, buf = refs[-3:]
    for d in ds:
        buf[:, at : at + d.shape[1]] = tn(a_ref[...], d[...])
        at += d.shape[1]
    mine = scal[bit]
    for m in range(buf.shape[0] // (2 * half)):
        own = pl.multiple_of(2 * half * m + half * mine, 8)
        other = pl.multiple_of(2 * half * m + half * (1 - mine), 8)
        keep[half * m : half * m + half, :] = buf[pl.ds(own, half), :].astype(BF16)
        send[half * m : half * m + half, :] = buf[pl.ds(other, half), :].astype(BF16)


def layer_specs(l, width):
    return [
        pl.BlockSpec((None, width, GC), lambda i, g: (l, 0, g)),
        pl.BlockSpec((None, width, GC), lambda i, g: (l, 0, g)),
        pl.BlockSpec((None, width, 2 * LANES), lambda i, g: (l, 0, 0)),
        pl.BlockSpec((None, width, LANES), lambda i, g: (l, 0, 0)),
        pl.BlockSpec((None, width, GC), lambda i, g: (l, 0, g)),
        pl.BlockSpec((None, 5, GC), lambda i, g: (l, 0, g)),
        pl.BlockSpec((None, 5, 2 * LANES), lambda i, g: (l, 0, 0)),
        pl.BlockSpec((None, 8, LANES), lambda i, g: (l, 0, 0)),
        pl.BlockSpec((None, 1, GC), lambda i, g: (l, 0, g)),
    ]


class Call:
    def __init__(self):
        self.in_specs, self.args, self.out_specs, self.out_shape = [], [], [], []
        self.aliases, self.tail = {}, []

    def take(self, spec, arg):
        self.in_specs.append(spec)
        self.args.append(arg)

    def give(self, spec, dims, dtype=F32, into=None):
        if into is not None:
            self.tail.append((into, len(self.out_specs)))
        self.out_specs.append(spec)
        self.out_shape.append(jax.ShapeDtypeStruct(dims, dtype))

    def run(self, kernel, grid, scratch, after, micros, name):
        for arg, out in self.tail:
            self.aliases[len(self.args)] = out
            self.take(pl.BlockSpec(memory_space=pl.ANY), arg)
        for arg in after:
            self.take(pl.BlockSpec(memory_space=pl.ANY), arg)
        return pl.pallas_call(
            functools.partial(kernel, len(self.tail) + len(after)),
            grid=grid,
            in_specs=self.in_specs,
            out_specs=self.out_specs,
            out_shape=self.out_shape,
            scratch_shapes=scratch,
            input_output_aliases=self.aliases,
            compiler_params=pltpu.CompilerParams(
                dimension_semantics=("arbitrary",) * len(grid), vmem_limit_bytes=VMEM_LIMIT
            ),
            cost_estimate=pl.CostEstimate(
                flops=int(micros * 1.1e9), bytes_accessed=1_000_000, transcendentals=0
            ),
            name=name,
        )(*self.args)


def full(dims, count):
    return pl.BlockSpec(dims, lambda *at: (0,) * count)


def smem():
    return pl.BlockSpec(memory_space=pltpu.SMEM)


def forward_call(l, chunk, chunks, half, inner, rows_all, scal, hid_prev, halves, halves_at, gains, weights, carry, filled, after):
    first, fresh = hid_prev is None, carry is None
    width = weights[0].shape[1]
    groups = weights[0].shape[2] // GC
    cols = groups * GC
    rows = chunks * Q

    def block(h, w, at=chunk):
        return pl.BlockSpec((h, w), lambda i, g: (at + i, 0))

    def grouped(h, w, at=chunk):
        return pl.BlockSpec((h, w), lambda i, g: (at + i, g))

    call = Call()
    call.take(smem(), scal)
    if not first:
        call.take(block(Q, width), hid_prev)
    for term in halves:
        call.take(block(Q // 2, term.shape[1], halves_at), term)
    call.take(full(gains.shape, 2), gains)
    for spec, arg in zip(layer_specs(l, width), weights):
        call.take(spec, arg)
    carry_shapes = [(groups, LANES, GC), (groups, 8, GC), (8, 2 * LANES)]
    if not fresh:
        for dims, arg in zip(carry_shapes, carry):
            call.take(full(dims, len(dims)), arg)
    into = filled if filled is not None else (None,) * 3
    call.give(block(Q, width), (rows_all, width), F32, into[0])
    call.give(block(Q, width), (rows_all, width), BF16, into[1])
    call.give(grouped(Q, GC), (rows_all, cols), BF16, into[2])
    call.give(grouped(Q, GC, 0), (rows, cols))
    call.give(grouped(Q, GC, 0), (rows, cols), BF16)
    call.give(grouped(Q, GC, 0), (rows, cols))
    call.give(grouped(Q, GC, 0), (rows, cols))
    call.give(block(Q, 2 * LANES, 0), (rows, 2 * LANES), BF16)
    call.give(block(Q, 2 * LANES, 0), (rows, 2 * LANES))
    call.give(block(Q, LANES, 0), (rows, LANES))
    call.give(
        pl.BlockSpec((None, None, LANES, GC), lambda i, g: (i, g, 0, 0)), (chunks, groups, LANES, GC)
    )
    for dims in carry_shapes:
        call.give(full(dims, len(dims)), dims)
    for _ in range(2):
        call.give(block(Q // 2, width + LANES, 0), (rows // 2, width + LANES))
    scratch = [
        pltpu.VMEM((Q, width + LANES), F32),
        pltpu.VMEM((Q, width + LANES), F32),
        pltpu.VMEM((Q, LANES), F32),
        pltpu.VMEM((Q + 8, GC), F32),
        pltpu.VMEM((Q + 8, 2 * LANES), F32),
        pltpu.VMEM((Q, LANES), BF16),
        pltpu.VMEM((Q, LANES), BF16),
        pltpu.VMEM((LANES, Q), BF16),
        pltpu.VMEM((Q, Q), F32),
        pltpu.VMEM((Q, LANES), F32),
        pltpu.VMEM((Q, LANES), F32),
        pltpu.VMEM((LANES, Q), F32),
    ]

    def kernel(n_skip, *refs):
        forward_kernel(first, fresh, n_skip, l, half, chunk * Q, inner, *refs)

    outs = call.run(kernel, (chunks, groups), scratch, after, 12 * chunks, "layer_forward")
    return tuple(outs[:3]), tuple(outs[3:11]), tuple(outs[11:14]), outs[14], outs[15]


def norm_call(l, top, bottom, chunk, chunks, half, inner, scal, hid, lead, lows, branch, gains, gain_c, filled, after):
    rows_all, width = hid.shape
    fresh = gain_c is None

    def block(h, w, at=chunk):
        return pl.BlockSpec((h, w), lambda i: (at + i, 0))

    call = Call()
    call.take(smem(), scal)
    call.take(block(Q, width), hid)
    call.take(block(Q, width), lead)
    if not top:
        for side in lows:
            call.take(block(Q // 2, width, 0), side)
    for side in branch:
        call.take(block(Q // 2, width + LANES, 0), side)
    call.take(full(gains.shape, 2), gains)
    if not fresh:
        call.take(full((8, width), 2), gain_c)
    into = filled if filled is not None else (None,) * 5
    if top:
        call.give(block(Q, width), (rows_all, width), BF16, into[4])
    part = 2 if bottom else 1
    call.give(block(Q // part, width), (rows_all // part, width), F32, into[0])
    call.give(block(Q, width), (rows_all, width), BF16, into[1])
    call.give(block(Q, width), (rows_all, width), BF16, into[2])
    call.give(block(Q, LANES), (rows_all, LANES), F32, into[3])
    call.give(full((8, width), 2), (8, width))
    scratch = [pltpu.VMEM((Q, width + LANES), F32), pltpu.VMEM((Q, width), F32)]

    def kernel(n_skip, *refs):
        norm_kernel(top, bottom, fresh, n_skip, l, half, chunk * Q, inner, *refs)

    outs = call.run(kernel, (chunks,), scratch, after, 4 * chunks, "norm_backward")
    result = None
    if top:
        result, outs = outs[0], outs[1:]
    return tuple(outs[:4]) + (result,), outs[4]


def backward_call(l, chunk, chunks, half, scal, gb, rows_f, weights, saved, carry, filled, after):
    width = weights[0].shape[1]
    groups = weights[0].shape[2] // GC
    cols = groups * GC
    rows, rows_all = chunks * Q, gb.shape[0]
    fresh = carry is None

    def block(h, w, at=chunk):
        return pl.BlockSpec((h, w), lambda i, g: (at + chunks - 1 - i, 0))

    def grouped(h, w, at=chunk):
        return pl.BlockSpec((h, w), lambda i, g: (at + chunks - 1 - i, g))

    call = Call()
    call.take(smem(), scal)
    call.take(block(Q, width), gb)
    call.take(block(Q, LANES), rows_f)
    for spec, arg in zip(layer_specs(l, width), weights):
        call.take(spec, arg)
    specs = [
        grouped(Q, GC, 0),
        grouped(Q, GC, 0),
        grouped(Q, GC, 0),
        grouped(Q, GC, 0),
        block(Q, 2 * LANES, 0),
        block(Q, 2 * LANES, 0),
        block(Q, LANES, 0),
        pl.BlockSpec((None, None, LANES, GC), lambda i, g: (chunks - 1 - i, g, 0, 0)),
    ]
    for spec, arg in zip(specs, saved):
        call.take(spec, arg)
    carry_shapes = [(groups, LANES, GC), (groups, 16, GC), (16, 2 * LANES), (8, LANES)]
    if not fresh:
        for dims, arg in zip(carry_shapes, carry):
            call.take(full(dims, len(dims)), arg)
    into = filled if filled is not None else (None,) * 4
    call.give(grouped(Q, GC), (rows_all, cols), BF16, into[0])
    call.give(grouped(Q, GC), (rows_all, cols), BF16, into[1])
    call.give(block(Q, 2 * LANES), (rows_all, 2 * LANES), BF16, into[2])
    call.give(block(Q, LANES), (rows_all, LANES), BF16, into[3])
    for _ in range(2):
        call.give(block(Q // 2, width, 0), (rows // 2, width))
    for dims in carry_shapes:
        call.give(full(dims, len(dims)), dims)
    scratch = [
        pltpu.VMEM((Q, width), F32),
        pltpu.VMEM((Q, Q), F32),
        pltpu.VMEM((Q, LANES), F32),
        pltpu.VMEM((Q, LANES), F32),
        pltpu.VMEM((Q + 8, GC), F32),
        pltpu.VMEM((Q + 8, 2 * LANES), F32),
        pltpu.VMEM((Q, LANES), BF16),
        pltpu.VMEM((Q, LANES), BF16),
        pltpu.VMEM((LANES, Q), BF16),
        pltpu.VMEM((Q, Q), F32),
        pltpu.VMEM((Q, LANES), F32),
        pltpu.VMEM((Q, LANES), F32),
        pltpu.VMEM((LANES, Q), F32),
        pltpu.VMEM((Q, LANES), F32),
        pltpu.VMEM((Q, LANES), F32),
        pltpu.VMEM((8, LANES), F32),
    ]

    def kernel(n_skip, *refs):
        backward_kernel(fresh, n_skip, l, half, *refs)

    outs = call.run(kernel, (chunks, groups), scratch, after, 16 * chunks, "layer_backward")
    return tuple(outs[:4]), outs[4], outs[5], tuple(outs[6:])


def weight_call(a, ds, piece, scal, bit, after):
    tokens, width = a.shape
    total = sum(d.shape[1] for d in ds)
    unit = piece * (bit or 1)
    step = 2 * unit
    while step < 384 and width % (2 * step) == 0:
        step *= 2
    call = Call()
    call.take(smem(), scal)
    call.take(pl.BlockSpec((tokens, step), lambda r: (0, r)), a)
    for d in ds:
        call.take(full(d.shape, 2), d)
    parts = 1 if bit is None else 2
    for _ in range(parts):
        call.give(pl.BlockSpec((step // parts, total), lambda r: (r, 0)), (width // parts, total), BF16)
    scratch = [] if bit is None else [pltpu.VMEM((step, total), F32)]

    def kernel(n_skip, *refs):
        weight_kernel(unit, None if bit is None else place_of(bit), len(ds), *refs)

    return call.run(kernel, (width // step,), scratch, after, total // 128, "weight_grad")


def pack_call(rows, wide, moves, after):
    call = Call()
    for src, _, _ in moves:
        call.take(pl.BlockSpec(memory_space=pltpu.VMEM), src)
    call.give(pl.BlockSpec(memory_space=pltpu.VMEM), (rows, wide))

    def kernel(n_skip, *refs):
        out = refs[-1]
        out[...] = jnp.zeros_like(out)
        for ref, (_, index, at) in zip(refs, moves):
            piece = ref[index]
            if piece.shape[1] <= wide:
                out[at : at + piece.shape[0], : piece.shape[1]] = piece
            else:
                for m in range(piece.shape[1] // wide):
                    out[at + m : at + m + 1, :] = piece[:, m * wide : (m + 1) * wide]

    return call.run(kernel, (), [], after, 2, "pack_small")[0]


def sum_call(a, b, after):
    call = Call()
    for arg in (a, b):
        call.take(pl.BlockSpec(memory_space=pltpu.VMEM), arg)
    call.give(pl.BlockSpec(memory_space=pltpu.VMEM), a.shape)

    def kernel(n_skip, x, y, *refs):
        refs[-1][...] = x[...] + y[...]

    return call.run(kernel, (), [], after, 1, "sum_small")[0]


def take_call(value, index, after):
    call = Call()
    call.take(smem(), index)
    call.take(pl.BlockSpec(memory_space=pltpu.VMEM), value)
    call.give(pl.BlockSpec(memory_space=pltpu.VMEM), value.shape, value.dtype)

    def kernel(n_skip, at, src, *refs):
        for k in range(value.shape[0]):
            refs[-1][k] = src[at[k]]

    return call.run(kernel, (), [], after, 2, "take_parts")[0]


class Butterfly:
    def __init__(self, value, steps):
        self.value, self.steps = value, list(steps)
        self.send()

    def send(self):
        if self.steps:
            self.came = swap(self.value, *self.steps.pop(0))
        else:
            self.came = None

    def step(self, after):
        self.value = sum_call(self.value, self.came, after)
        self.send()
        return self.value


def pairs(axis, bit):
    return [(i, i ^ bit) for i in range(lax.axis_size(axis))]


def swap(value, axis, bit):
    return lax.ppermute(value, axis, pairs(axis, bit))


def sum_pairs(value, axis, bit):
    return value + swap(value, axis, bit)


def place_of(bit):
    return 1 + bit.bit_length() + (bit >= 4)


class Scatter:
    def __init__(self, keep, send, piece, order):
        self.keep, self.recv, self.piece = keep, swap(send, "dp", order[0]), piece
        self.order, self.left = list(order[1:]), sorted(order[1:])

    def step(self, scal, after):
        bit = self.order.pop(0)
        unit = self.piece << self.left.index(bit)
        self.left.remove(bit)
        self.keep, send = scatter_call(self.keep, self.recv, unit, place_of(bit), scal, after)
        self.recv = swap(send, "dp", bit)
        return send


def finish_call(items, after):
    call = Call()
    count = 0
    for scatter, upper, parts in items:
        rows = scatter.keep.shape[0]
        for arg in (scatter.keep, scatter.recv):
            call.take(pl.BlockSpec(arg.shape, lambda r: (0, 0)), arg)
        for wide, at in parts:
            call.take(pl.BlockSpec((rows, wide), lambda r, j=at // wide: (0, j)), upper)
            call.give(pl.BlockSpec((2, rows, wide), lambda r: (0, 0, 0)), (2, rows, wide))
            count += 1

    def kernel(n_skip, *refs):
        it, out = iter(refs), iter(refs[len(refs) - count :])
        for _, _, parts in items:
            a, b, at = next(it), next(it), 0
            for wide, _ in parts:
                cols = slice(at, at + wide)
                dst = next(out)
                dst[0] = a[:, cols].astype(F32) + b[:, cols].astype(F32)
                dst[1] = next(it)[...].astype(F32)
                at += wide

    return call.run(kernel, (1,), [], after, 3, "finish")


def own_part(rows, half, place):
    parts = rows.reshape(-1, 2, half // 2, rows.shape[1])
    return lax.dynamic_index_in_dim(parts, place, axis=1, keepdims=False).reshape(-1, rows.shape[1])


def add_call(keep, recv, width, after):
    rows, wide = keep.shape
    call = Call()
    spec = pl.BlockSpec((rows // 2, wide), lambda r: (r, 0))
    call.take(spec, keep)
    call.take(spec, recv)
    call.give(spec, (rows, wide), BF16)

    def kernel(n_skip, a, b, *refs):
        out = refs[-1]
        total = a[...] + b[...]
        if wide == width:
            out[...] = total.astype(BF16)
        else:
            out[:, :width] = total[:, :width].astype(BF16)
            tail = total[:, width:]
            lead = tail.astype(BF16).astype(F32)
            lane = lax.broadcasted_iota(jnp.int32, tail.shape, 1)
            out[:, width:] = jnp.where(lane < P_SIZE, lead, tail - lead).astype(BF16)

    return call.run(kernel, (2,), [], after, 2, "add_pair")[0]


def add_quarter_call(keep, recv, half, scal, after):
    rows, wide = keep.shape
    unit = half // 2
    call = Call()
    call.take(smem(), scal)
    for arg in (keep, recv):
        call.take(pl.BlockSpec(memory_space=pltpu.VMEM), arg)
    call.give(pl.BlockSpec(memory_space=pltpu.VMEM), (rows // 2, wide))
    call.give(pl.BlockSpec(memory_space=pltpu.VMEM), (rows // 2, wide), BF16)

    def kernel(n_skip, place_ref, a, b, *refs):
        mine, other, buf = refs[-3:]
        place = place_ref[4]
        for m in range(rows // half):
            for dst, side in ((mine, place), (buf, 1 - place)):
                at = pl.multiple_of(half * m + unit * side, 8)
                dst[unit * m : unit * m + unit, :] = a[pl.ds(at, unit), :] + b[pl.ds(at, unit), :]
        other[...] = buf[...].astype(BF16)

    return call.run(kernel, (), [pltpu.VMEM((rows // 2, wide), F32)], after, 2, "add_quarter")


def last_call(mine, other, d_hid, x_mine, chunk, half, scal, gains, gain_c, filled, after):
    rows, wide = mine.shape
    unit = half // 2
    fresh = gain_c is None
    call = Call()
    call.take(smem(), scal)
    part = pl.BlockSpec((rows, wide), lambda r: (0, 0))
    whole = pl.BlockSpec((2 * rows, wide), lambda r: (chunk, 0))
    for spec, arg in ((part, mine), (part, other), (whole, d_hid), (whole, x_mine)):
        call.take(spec, arg)
    call.take(full(gains.shape, 2), gains)
    if not fresh:
        call.take(full((8, wide), 2), gain_c)
    call.give(pl.BlockSpec((rows, wide), lambda r: (chunk, 0)), (d_hid.shape[0] // 2, wide), BF16, filled)
    call.give(full((8, wide), 2), (8, wide))

    def kernel(n_skip, place_ref, a, b, dh_ref, x_ref, gain_ref, *refs):
        out, gain_acc, x_s, x_q, dh_q = refs[-5:]
        place = place_ref[4]
        x_s[...] = x_ref[...].astype(F32)
        for m in range(rows // unit):
            at = pl.multiple_of(half * m + unit * place, 8)
            dst = slice(unit * m, unit * m + unit)
            token = chunk * Q + (2 * half) * m + half * place_ref[0] + unit * place
            token = token + lax.broadcasted_iota(jnp.int32, (unit, 1), 0)
            x_q[dst, :] = jnp.where(token < place_ref[1], x_s[pl.ds(at, unit), :], 0.0)
            dh_q[dst, :] = jnp.where(token < place_ref[1], dh_ref[pl.ds(at, unit), :], 0.0)
        hid = x_q[...]
        r = lax.rsqrt(row_mean(hid * hid) + EPS)
        normed = hid * r
        upper = a[...] + b[...].astype(F32)
        gain_acc[...] = jnp.zeros_like(gain_acc) if fresh else refs[0][...]
        gain_acc[0:1, :] += col_sum(upper * normed)
        dn = upper * gain_ref[0:1, :]
        back = r * (dn - normed * row_mean(dn * normed))
        out[...] = (dh_q[...] + back).astype(BF16)

    scratch = [
        pltpu.VMEM((2 * rows, wide), F32),
        pltpu.VMEM((rows, wide), F32),
        pltpu.VMEM((rows, wide), F32),
    ]
    return call.run(kernel, (1,), scratch, after, 4, "norm_last")


def scatter_call(keep, recv, unit, place_at, scal, after):
    rows, wide = keep.shape
    call = Call()
    call.take(smem(), scal)
    spec = pl.BlockSpec((2 * unit, wide), lambda r: (r, 0))
    call.take(spec, keep)
    call.take(spec, recv)
    for _ in range(2):
        call.give(pl.BlockSpec((unit, wide), lambda r: (r, 0)), (rows // 2, wide), BF16)

    def kernel(n_skip, place_ref, a, b, *refs):
        own = place_ref[place_at]
        for dst, side in ((refs[-2], own), (refs[-1], 1 - own)):
            at = pl.ds(pl.multiple_of(unit * side, 16), unit)
            dst[...] = (a[at, :].astype(F32) + b[at, :].astype(F32)).astype(BF16)

    return call.run(kernel, (rows // (2 * unit),), [], after, 3, "add_scatter")


class Offload:
    def __init__(self, value):
        self.value = lax.psum_scatter(value, "dp", scatter_dimension=0, tiled=True)


class Sums:
    def __init__(self, width, half, scal):
        self.width, self.half, self.scal, self.open = width, half, scal, []

    def start(self, keep, send):
        self.open.insert(0, [keep, swap(send, "tensor", 1), None, None])

    def add(self, entry, after):
        keep, recv = entry[0], entry[1]
        own = add_call(keep, recv, self.width, after)
        other = swap(own, "tensor", 2)
        entry[2] = own
        entry[3] = (own, other, swap(own, "tensor", 1), swap(other, "tensor", 1))
        return own

    def add_quarter(self, entry, after):
        mine, other = add_quarter_call(entry[0], entry[1], self.half, self.scal, after)
        entry[2] = other
        entry[3] = (mine, swap(other, "tensor", 2))
        return other


def per_device(
    x_in,
    cotangent,
    lengths,
    deal_order,
    norm_gains,
    proj_gate,
    proj_value,
    proj_state,
    proj_step,
    proj_out,
    conv_value,
    conv_state,
    step_bias,
    decay_log,
    skip_gain,
    inner_gain,
):
    _, slot_len, width = cotangent.shape
    layers = proj_gate.shape[0]
    cols = proj_gate.shape[2]
    heads = step_bias.shape[1]
    inner = cols * lax.axis_size("tensor")
    dp = lax.axis_size("dp")
    half = x_in.shape[1] // 2
    piece = width // dp
    me = lax.axis_index("dp")
    core = lax.rem(lax.axis_index("tensor"), 2)
    length = jnp.take(lengths, lax.dynamic_index_in_dim(deal_order, me, keepdims=False))
    place = lax.axis_index("tensor") // 2
    bits = [1 << k for k in range(dp.bit_length() - 1)]
    parts = [lax.rem(me // bit, 2) for bit in bits]
    scal = jnp.stack([core, length] + parts[:2] + [place] + parts[2:]).astype(jnp.int32)

    x_half = lax.dynamic_slice_in_dim(x_in, core * half, half, axis=1)
    x_dealt = jnp.take(x_half, deal_order, axis=0)
    x_mine = lax.all_to_all(x_dealt, "dp", split_axis=0, concat_axis=0, tiled=True)
    x_mine = x_mine.reshape(slot_len // 2, width)
    x_theirs = swap(x_mine, "tensor", 1)

    heads_p = jnp.pad(
        jnp.stack([step_bias, decay_log, skip_gain], axis=1), ((0, 0), (0, 5), (0, LANES - heads))
    )
    weights = (
        proj_gate,
        proj_value,
        proj_state,
        jnp.pad(proj_step, ((0, 0), (0, 0), (0, LANES - heads))),
        proj_out,
        conv_value,
        conv_state,
        heads_p,
        inner_gain[:, None, :],
    )
    cot = cotangent.reshape(slot_len, width)
    sums = Sums(width, half, scal)
    calls = slot_len // (Q * CHUNKS)

    def due(entries, prior):
        if len(entries) > 1 and entries[1][2] is None:
            entries_add(entries[1], [prior])
        return [entries[1][2]] if len(entries) > 1 else []

    entries_add = sums.add
    filled_f, saves, branches = [], [], []
    prior = None
    for l in range(layers):
        carry, filled, save_l, branch_l = None, None, [], []
        for c in range(calls):
            if l == 0:
                lead = (None, (x_mine, x_theirs), c * CHUNKS)
            else:
                lead = (filled_f[l - 1][0], branches[l - 1][c][3], 0)
            after = due(sums.open, prior)
            if len(sums.open) > 2:
                after.append(sums.open[2][3][1])
            filled, saved, carry, keep, send = forward_call(
                l, c * CHUNKS, CHUNKS, half, inner, slot_len, scal, *lead, norm_gains, weights, carry, filled, after
            )
            prior = keep
            save_l.append(saved)
            sums.start(keep, send)
            branch_l.append(sums.open[0])
        filled_f.append(filled)
        saves.append(save_l)
        branches.append(branch_l)
    for entry in (sums.open[1], sums.open[0]):
        if entry[2] is None:
            prior = sums.add(entry, [prior])

    swapped = [bits[1], bits[0]] + bits[2:]
    lows = [(None,) * 4] * calls
    filled_n = None
    smalls, g_outs, g_ins = [], [], []
    for l in reversed(range(layers)):
        top, bottom = l == layers - 1, l == 0
        order = list(range(calls)) if top else list(reversed(range(calls)))
        lead = cot if top else filled_n[0]
        hid = filled_f[l][0] if top else filled_f[l + 1][0]
        filled_n, gain_c = None, None
        for c in order:
            after = [prior] if c == order[0] else []
            filled_n, gain_c = norm_call(
                l, top, bottom, c * CHUNKS, CHUNKS, half, inner, scal, hid, lead, lows[c][3] if not top else None, branches[l][c][3], norm_gains, gain_c, filled_n, after
            )
        if top:
            result = filled_n[4]
        _, low_all, u_all = filled_f[l]
        carry, filled, new_lows = None, None, [None] * calls
        sums.open = []
        if bottom:
            out_keep, out_send = weight_call(filled_n[2], [u_all], piece, scal, bits[0], [])
            out = Scatter(out_keep, out_send, piece, bits)
            entries_add = sums.add_quarter
            last, gain_first = None, None
        else:
            out_send = weight_call(filled_n[2], [u_all], piece, scal, None, [])[0]
            out = Offload(out_send)
        g_outs.insert(0, out)
        prior = out_send
        for at, c in enumerate(reversed(range(calls))):
            after = due(sums.open, prior)
            if not sums.open:
                after = [out_send]
            if bottom:
                if at >= 3:
                    after.append(out.step(scal, [after[0]]))
                if at >= 2 and len(sums.open) > 2:
                    last, gain_first = last_call(
                        *sums.open[2][3], filled_n[0], x_mine, (c + 3) * CHUNKS, half, scal, norm_gains, gain_first, last, [prior]
                    )
                    after.append(gain_first)
            elif len(sums.open) > 2:
                after.append(sums.open[2][3][1])
            filled, keep, send, carry = backward_call(
                l, c * CHUNKS, CHUNKS, half, scal, filled_n[1], filled_n[3], weights, saves[l][c], carry, filled, after
            )
            prior = keep
            sums.start(keep, send)
            new_lows[c] = sums.open[0]
        lows = new_lows
        _, acc_v, acc_s, acc_h = carry
        smalls.insert(0, (acc_v, acc_s, acc_h, gain_c))
        d_gate, d_val, d_st, d_step = filled
        if not bottom:
            prior = sums.add(sums.open[1], [prior])
            prior = sums.add(sums.open[0], [prior])
            after = [prior, out.value]
            prior = weight_call(low_all, [d_val, d_gate, d_st, d_step], piece, scal, None, after)[0]
            g_ins.insert(0, Offload(prior))

    def finish_rows(entry, chunk, after):
        return last_call(
            *entry[3], filled_n[0], x_mine, chunk * CHUNKS, half, scal, norm_gains, gain_first, last, after
        )

    groups = cols // GC
    gain_rows = width // GC
    dp_steps = [("dp", bit) for bit in bits]
    prior = sums.add_quarter(sums.open[1], [prior])
    last, gain_first = finish_rows(sums.open[2], 2, [prior])
    per_layer = groups * 8 + 8 + 8 * ((gain_rows + 7) // 8)
    moves = []
    for l, (acc_v, _, acc_h, gain) in enumerate(smalls):
        for g in range(groups):
            moves.append((acc_v, (g, slice(0, 8)), l * per_layer + 8 * g))
        moves.append((acc_h, slice(0, 8), l * per_layer + 8 * groups))
        moves.append((gain, slice(0, 1), l * per_layer + 8 * groups + 8))
    small = Butterfly(pack_call(layers * per_layer, GC, moves, [gain_first]), dp_steps)
    prior = sums.add_quarter(sums.open[0], [small.value])
    prior = small.step([prior])
    while out.order:
        prior = out.step(scal, [prior])
    val_keep, val_send = weight_call(low_all, [d_val], piece, scal, bits[0], [prior])
    val = Scatter(val_keep, val_send, piece, bits)
    last, gain_first = finish_rows(sums.open[1], 1, [val_send])
    prior = small.step([gain_first])
    last, gain_first = finish_rows(sums.open[0], 0, [prior])
    rows = 8 * layers
    moves = [(acc_s, slice(0, 8), 8 * l) for l, (_, acc_s, _, _) in enumerate(smalls)]
    moves.append((gain_first, slice(0, 1), rows))
    rest_small = Butterfly(
        pack_call(rows + 8 * ((gain_rows + 7) // 8), GC, moves, []),
        [("tensor", 1), ("tensor", 2)] + dp_steps,
    )
    misc_keep, misc_send = weight_call(low_all, [d_st, d_step], piece, scal, swapped[0], [rest_small.value])
    misc = Scatter(misc_keep, misc_send, piece, swapped)
    prior = rest_small.step([misc_send])
    while small.came is not None:
        prior = small.step([prior])
    gate_keep, gate_send = weight_call(low_all, [d_gate], piece, scal, swapped[0], [prior])
    gate = Scatter(gate_keep, gate_send, piece, swapped)
    quarter = half // 2
    grad_in = last.reshape(dp, quarter, width)
    returned = lax.all_to_all(grad_in, "dp", split_axis=0, concat_axis=0, tiled=True)
    places = jnp.arange(dp)
    inverse = jnp.sum(jnp.where(deal_order[None, :] == places[:, None], places[None, :], 0), axis=1)
    arrived = take_call(returned, inverse.astype(jnp.int32), [gate_send])
    prior = misc.step(scal, [arrived])
    prior = val.step(scal, [prior])
    prior = rest_small.step([prior])
    prior = gate.step(scal, [prior])

    def side_by_side(mine, theirs, first):
        return jnp.where(
            first == 0,
            jnp.concatenate([mine, theirs], axis=1),
            jnp.concatenate([theirs, mine], axis=1),
        )

    joined = side_by_side(arrived, swap(arrived, "tensor", 2), place)
    grad_x = side_by_side(joined, swap(joined, "tensor", 1), core)

    upper = g_ins[0].value
    prior = misc.step(scal, [prior, joined])
    prior = val.step(scal, [prior])
    prior = gate.step(scal, [prior])
    prior = rest_small.step([prior])
    while gate.order:
        for scatter in (misc, val, gate):
            prior = scatter.step(scal, [prior])
    g_state, g_step = finish_call(
        [(misc, upper, [(2 * LANES, 2 * cols), (LANES, 2 * cols + 2 * LANES)])], [prior]
    )
    for bit in (1, 2):
        g_state = sum_pairs(g_state, "tensor", bit)
    prior = g_step
    while rest_small.came is not None:
        prior = rest_small.step([prior])
    g_out, g_value, g_gate = finish_call(
        [(out, g_outs[1].value, [(cols, 0)]), (val, upper, [(cols, 0)]), (gate, upper, [(cols, cols)])],
        [prior],
    )
    small, rest_small = small.value, rest_small.value
    small = small.reshape(layers, per_layer, GC)
    v_sum = jnp.swapaxes(small[:, : groups * 8].reshape(layers, groups, 8, GC), 1, 2)
    v_sum = v_sum.reshape(layers, 8, cols)
    h_sum = small[:, groups * 8 : groups * 8 + 2, :heads]
    gain_sum = small[:, groups * 8 + 8 : groups * 8 + 8 + gain_rows].reshape(layers, width)
    s_sum = rest_small[:rows].reshape(layers, 8, GC)[:, :5]
    gain_first = rest_small[rows : rows + gain_rows].reshape(1, width)
    gain_own = lax.dynamic_slice_in_dim(
        jnp.concatenate([gain_first, gain_sum], axis=0), me * piece, piece, axis=1
    )

    skip_grad = v_sum[:, 6].reshape(layers, heads, P_SIZE).sum(axis=2)
    return (
        result[None],
        grad_x,
        gain_own,
        g_gate,
        g_value,
        g_state,
        g_step[:, :, :heads],
        g_out,
        v_sum[:, :5],
        s_sum,
        h_sum[:, 0],
        h_sum[:, 1],
        skip_grad,
        v_sum[:, 5],
    )


def solution(mesh):
    return jax.shard_map(
        per_device,
        mesh=mesh,
        in_specs=(
            P(None, "dp", None),
            P("dp", None, None),
            P(),
            P(),
            P(),
            P(None, None, "tensor"),
            P(None, None, "tensor"),
            P(),
            P(None, None, "tensor"),
            P(None, None, "tensor"),
            P(None, None, "tensor"),
            P(),
            P(None, "tensor"),
            P(None, "tensor"),
            P(None, "tensor"),
            P(None, "tensor"),
        ),
        out_specs=(
            P("dp", None, None),
            P(None, "dp", None),
            P(None, "dp"),
            P(None, "dp", "tensor"),
            P(None, "dp", "tensor"),
            P(None, "dp", None),
            P(None, "dp", "tensor"),
            P(None, "dp", "tensor"),
            P(None, None, "tensor"),
            P(),
            P(None, "tensor"),
            P(None, "tensor"),
            P(None, "tensor"),
            P(None, "tensor"),
        ),
        check_vma=False,
    )
```

```python
import functools

import jax
import jax.numpy as jnp
from jax import lax
from jax.experimental import pallas as pl
from jax.experimental.pallas import tpu as pltpu
from jax.sharding import PartitionSpec as P

P_SIZE = 64
Q = 256
R = 128
GC = 256
HG = GC // P_SIZE
LANES = 128
EPS = 1e-05
CHUNKS = 1
VMEM_LIMIT = 44 * 1024 * 1024
VMEM_SMALL = 24 * 1024 * 1024

F32 = jnp.float32
BF16 = jnp.bfloat16


def nn(a, b):
    return jnp.dot(a, b, preferred_element_type=F32)


def nt(a, b):
    return lax.dot_general(a, b, (((1,), (1,)), ((), ())), preferred_element_type=F32)


def tn(a, b):
    return lax.dot_general(a, b, (((0,), (0,)), ((), ())), preferred_element_type=F32)


def exact(a, b):
    return jnp.dot(a, b, preferred_element_type=F32, precision=lax.Precision.HIGHEST)


def sigmoid(v):
    return 1.0 / (1.0 + jnp.exp(-v))


def softplus(v):
    return jnp.maximum(v, 0.0) + jnp.log1p(jnp.exp(-jnp.abs(v)))


def triangle(lower):
    rows = lax.broadcasted_iota(jnp.int32, (Q, Q), 0)
    cols = lax.broadcasted_iota(jnp.int32, (Q, Q), 1)
    return rows >= cols if lower else cols >= rows


def row_mean(v):
    return jnp.mean(v, axis=1, keepdims=True)


def col_sum(v):
    return jnp.sum(v, axis=0, keepdims=True)


def join_halves(dst, mine, theirs, core, half):
    width = mine[0].shape[-1]
    for m in range(dst.shape[0] // (2 * half)):
        rows = slice(half * m, half * m + half)
        for terms, side in ((mine, core), (theirs, 1 - core)):
            total = terms[0][rows, :].astype(F32)
            for term in terms[1:]:
                total = total + term[rows, :].astype(F32)
            dst[pl.ds(pl.multiple_of(2 * half * m + half * side, 8), half), :width] = total


def join_quarters(dst, parts, core, place, half):
    width, unit = parts[0].shape[-1], half // 2
    for m in range(dst.shape[0] // (2 * half)):
        for k, part in enumerate(parts):
            side = (core, 1 - core)[k // 2]
            along = (place, 1 - place)[k % 2]
            at = pl.multiple_of(2 * half * m + half * side + unit * along, 8)
            dst[pl.ds(at, unit), :width] = part[unit * m : unit * m + unit, :].astype(F32)


def split_halves(src, keep, send, core, half):
    width = keep.shape[-1]
    for m in range(src.shape[0] // (2 * half)):
        own = pl.multiple_of(2 * half * m + half * core, 8)
        keep[half * m : half * m + half, :] = src[pl.ds(own, half), :width].astype(keep.dtype)
        if send is not None:
            other = pl.multiple_of(2 * half * m + half * (1 - core), 8)
            send[half * m : half * m + half, :] = src[pl.ds(other, half), :width].astype(send.dtype)


def spread(per_head):
    rows = per_head.shape[0]
    lane = lax.broadcasted_iota(jnp.int32, (rows, LANES), 1)
    tiles = []
    for q in range(GC // LANES):
        left = jnp.broadcast_to(per_head[:, 2 * q : 2 * q + 1], (rows, LANES))
        right = jnp.broadcast_to(per_head[:, 2 * q + 1 : 2 * q + 2], (rows, LANES))
        tiles.append(jnp.where(lane < P_SIZE, left, right))
    return jnp.concatenate(tiles, axis=1)


def to_group(per_head, group):
    return pltpu.roll(per_head, lax.rem(LANES - group * HG, LANES), 1)


def skip_row(heads_p, group):
    return spread(to_group(jnp.broadcast_to(heads_p[2:3, :], (8, LANES)), group))[0:1, :]


def head_part(tile, parity):
    lane = lax.broadcasted_iota(jnp.int32, tile.shape, 1)
    return jnp.where((lane < P_SIZE) == (parity == 0), tile, jnp.zeros_like(tile))


def gather_heads(acc, cols, group):
    lane = lax.broadcasted_iota(jnp.int32, (cols.shape[0], LANES), 1)
    for j in range(HG):
        tile = head_part(cols[:, (j // 2) * LANES : (j // 2 + 1) * LANES], j % 2)
        total = jnp.sum(tile, axis=1, keepdims=True)
        acc = acc + jnp.where(lane == group * HG + j, total, 0.0)
    return acc


def two_terms(column):
    lead = column.astype(BF16).astype(F32)
    lane = lax.broadcasted_iota(jnp.int32, (column.shape[0], LANES), 1)
    return jnp.where(lane < P_SIZE, lead, column - lead)


def conv_rows(buf, taps):
    out = taps[4:5, :] + taps[0:1, :] * buf[5 : 5 + Q, :]
    for k in range(1, 4):
        out = out + taps[k : k + 1, :] * buf[5 + k : 5 + k + Q, :]
    return out


class Fetch:
    def __init__(self, l, refs, bufs, sems):
        self.l, self.refs, self.bufs, self.sems = l, refs, bufs, sems
        self.groups = bufs[0].shape[0]

    def grouped(self, kind, group):
        src = self.refs[kind].at[self.l, :, pl.ds(pl.multiple_of(group * GC, GC), GC)]
        return pltpu.make_async_copy(src, self.bufs[kind].at[group], self.sems.at[kind, group])

    def single(self, kind):
        return pltpu.make_async_copy(self.refs[kind].at[self.l], self.bufs[kind], self.sems.at[kind, 0])

    def start(self, order, singles_first):
        if singles_first:
            for kind in (3, 4):
                self.single(kind).start()
        for group in range(self.groups):
            for kind in order:
                self.grouped(kind, group).start()
        if not singles_first:
            for kind in (3, 4):
                self.single(kind).start()


def fetch_scratch(width, groups):
    return [
        pltpu.VMEM((groups, width, GC), BF16),
        pltpu.VMEM((groups, width, GC), BF16),
        pltpu.VMEM((groups, width, GC), BF16),
        pltpu.VMEM((width, 2 * LANES), BF16),
        pltpu.VMEM((width, LANES), BF16),
        pltpu.SemaphoreType.DMA((5, groups)),
    ]


def forward_kernel(first_layer, fresh, n_skip, l, half, base, inner, scal, *refs):
    it = iter(refs)
    if not first_layer:
        hid_prev = next(it)
    mine = [next(it), next(it)]
    theirs = [next(it), next(it)]
    gains = next(it)
    w_gate, w_value, w_state, w_step, w_out = (next(it) for _ in range(5))
    taps_v, taps_s, heads_p, gain_in = (next(it) for _ in range(4))
    if not fresh:
        h_in, vt_in, st_in = (next(it) for _ in range(3))
    for _ in range(n_skip):
        next(it)
    hid_hbm, low_hbm, u_out = next(it), next(it), next(it)
    if not first_layer:
        br_out = next(it)
    gate_out, vin_out, cv_out, y_out, sin_out, cs_out, dt_out, hs_out = (next(it) for _ in range(8))
    h_last, vt_last, st_last, keep, send = (next(it) for _ in range(5))
    buf, acc, sq, vbuf, sbuf, b_s, c_s, bt_s, s_s, step_s, cum_s, cumt_s = (
        next(it) for _ in range(12)
    )
    low_out, out_sems = next(it), next(it)
    bufs = [next(it) for _ in range(5)]
    fetch = Fetch(l, (w_gate, w_value, w_out, w_state, w_step), bufs, next(it))
    gain = gains[l : l + 1, :]
    bias, decay_log = heads_p[0:1, :], heads_p[1:2, :]

    i, g = pl.program_id(0), pl.program_id(1)
    core = scal[0]
    width = low_out.shape[1]

    def stores():
        rows = pl.ds(pl.multiple_of(base + i * Q, Q), Q)
        return (
            pltpu.make_async_copy(buf.at[:, pl.ds(0, width)], hid_hbm.at[rows], out_sems.at[0]),
            pltpu.make_async_copy(low_out, low_hbm.at[rows], out_sems.at[1]),
        )

    @pl.when(g == 0)
    def _():
        @pl.when(i == 0)
        def _():
            fetch.start((0, 1, 2), True)
            if fresh:
                h_last[...] = jnp.zeros_like(h_last)
                vt_last[...] = jnp.zeros_like(vt_last)
                st_last[...] = jnp.zeros_like(st_last)
            else:
                h_last[...] = h_in[...]
                vt_last[...] = vt_in[...]
                st_last[...] = st_in[...]

        if first_layer:
            join_quarters(buf, mine + theirs, core, scal[4], half)
        else:
            join_halves(buf, mine, theirs, core, half)
        if first_layer:
            token = base + i * Q + lax.broadcasted_iota(jnp.int32, (Q, 1), 0)
            hid = jnp.where(token < scal[1], buf[:, :width], 0.0)
        else:
            total = buf[:, width : width + 1] + buf[:, width + P_SIZE : width + P_SIZE + 1]
            br_out[:, :width] = buf[:, :width].astype(BF16)
            br_out[:, width:] = two_terms(total).astype(BF16)
            hid = hid_prev[...] + lax.rsqrt(total / inner + EPS) * buf[:, :width]
        buf[:, :width] = hid
        low_out[...] = (hid * lax.rsqrt(row_mean(hid * hid) + EPS) * gain).astype(BF16)
        for copy in stores():
            copy.start()
        low = low_out[...]

        @pl.when(i == 0)
        def _():
            fetch.single(3).wait()
            fetch.single(4).wait()

        s_in = nn(low, bufs[3][...])
        sin_out[...] = s_in.astype(BF16)
        sbuf[0:8, :] = st_last[...]
        sbuf[8 : 8 + Q, :] = s_in
        st_last[...] = s_in[Q - 8 : Q, :]
        cs = conv_rows(sbuf, taps_s)
        cs_out[...] = cs
        states = cs * sigmoid(cs)
        b_val, c_val = states[:, :LANES], states[:, LANES:]
        b_s[...] = b_val.astype(BF16)
        c_s[...] = c_val.astype(BF16)
        bt_s[...] = b_val.T.astype(BF16)
        s_s[...] = nt(c_s[...], b_s[...])
        dt = nn(low, bufs[4][...])
        dt_out[...] = dt
        step = softplus(dt + bias)
        cum = -exact(triangle(True).astype(F32), step * jnp.exp(decay_log))
        step_s[...] = step
        cum_s[...] = cum
        cumt_s[...] = cum.T
        acc[...] = jnp.zeros_like(acc)
        sq[...] = jnp.zeros_like(sq)

    @pl.when(i == 0)
    def _():
        fetch.grouped(0, g).wait()
        fetch.grouped(1, g).wait()

    low = low_out[...]
    gate = nn(low, bufs[0][g])
    gate_out[...] = gate.astype(BF16)
    v_in = nn(low, bufs[1][g])
    vin_out[...] = v_in.astype(BF16)
    vbuf[0:8, :] = vt_last[g]
    vbuf[8 : 8 + Q, :] = v_in
    vt_last[g] = v_in[Q - 8 : Q, :]
    cv = conv_rows(vbuf, taps_v)
    cv_out[...] = cv
    val = cv * sigmoid(cv)
    cum_g = to_group(cum_s[...], g)
    step_g = to_group(step_s[...], g)
    cum_e = spread(cum_g)
    scaled = spread(step_g) * val
    scaled_b = scaled.astype(BF16)
    h_enter = h_last[g]
    hs_out[...] = h_enter
    y = nn(c_s[...], h_enter.astype(BF16)) * jnp.exp(cum_e)
    end = cum_e[Q - 1 : Q, :]
    to_end = (scaled * jnp.exp(end - cum_e)).astype(BF16)
    h_last[g] = h_enter * jnp.exp(end) + nn(bt_s[...], to_end)
    causal = triangle(True)
    tiles = []
    for q in range(GC // LANES):
        tile = jnp.zeros((Q, LANES), F32)
        for parity in range(2):
            j = 2 * q + parity
            gaps = cum_g[:, j : j + 1] - cumt_s[pl.ds(g * HG + j, 1), :]
            weights = jnp.exp(jnp.where(causal, gaps, -1e30))
            mix = (s_s[...] * weights).astype(BF16)
            tile = tile + nn(mix, head_part(scaled_b[:, q * LANES : (q + 1) * LANES], parity))
        tiles.append(tile)
    y = y + jnp.concatenate(tiles, axis=1)
    y_out[...] = y
    gated = (y + skip_row(heads_p, g) * val) * (gate * sigmoid(gate))
    sq[...] += jnp.sum(gated * gated, axis=1, keepdims=True)
    u_out[...] = (gated * gain_in[...]).astype(BF16)

    @pl.when(i == 0)
    def _():
        fetch.grouped(2, g).wait()

    acc[:, :width] += nt(u_out[...], bufs[2][g])

    @pl.when(g == pl.num_programs(1) - 1)
    def _():
        acc[:, width:] = two_terms(sq[:, 0:1])
        split_halves(acc, keep, send, core, half)
        for copy in stores():
            copy.wait()


def norm_kernel(top, bottom, fresh, n_skip, l, half, base, inner, scal, *refs):
    it = iter(refs)
    hid_ref = next(it)
    if top:
        cot = next(it)
    else:
        dh_prev = next(it)
        dl_mine, dl_theirs = ([next(it), next(it)] for _ in range(2))
    if top:
        br_mine, br_theirs = ([next(it), next(it)] for _ in range(2))
    else:
        br_ref = next(it)
    gains = next(it)
    if not fresh:
        gain_c = next(it)
    for _ in range(n_skip):
        next(it)
    if top:
        result = next(it)
    dh_out, gb_out, gbs_out, rows_out, gain_acc, buf, low = (next(it) for _ in range(7))
    core = scal[0]
    width = gb_out.shape[1]
    gain = gains[l + 1 : l + 2, :]

    @pl.when(pl.program_id(0) == 0)
    def _():
        gain_acc[...] = jnp.zeros_like(gain_acc) if fresh else gain_c[...]

    if top:
        join_halves(buf, br_mine, br_theirs, core, half)
    else:
        buf[...] = br_ref[...].astype(F32)
    total = buf[:, width : width + 1] + buf[:, width + P_SIZE : width + P_SIZE + 1]
    scale = lax.rsqrt(total / inner + EPS)
    hid = hid_ref[...]
    if top:
        hid = hid + scale * buf[:, :width]
    r = lax.rsqrt(row_mean(hid * hid) + EPS)
    normed = hid * r
    if top:
        token = base + pl.program_id(0) * R + lax.broadcasted_iota(jnp.int32, (R, 1), 0)
        valid = token < scal[1]
        result[...] = jnp.where(valid, normed * gain, 0.0).astype(BF16)
        upper = jnp.where(valid, cot[...].astype(F32), 0.0)
    else:
        join_halves(low, dl_mine, dl_theirs, core, half)
        upper = low[...]
    gain_acc[0:1, :] += col_sum(upper * normed)
    dn = upper * gain
    dh = r * (dn - normed * row_mean(dn * normed))
    if not top:
        dh = dh + dh_prev[...]
    gb = dh.astype(BF16)
    gb_out[...] = gb
    gbs_out[...] = (dh * scale).astype(BF16)
    stat = jnp.sum(gb.astype(F32) * buf[:, :width], axis=1, keepdims=True)
    lane = lax.broadcasted_iota(jnp.int32, (R, LANES), 1)
    rows_out[...] = jnp.where(lane == 0, scale, scale * scale * scale * stat / inner)
    if bottom:
        low[...] = dh
        split_halves(low, dh_out, None, core, half)
    else:
        dh_out[...] = dh


def backward_kernel(fresh, n_skip, l, half, scal, *refs):
    it = iter(refs)
    gb_ref, rows_ref = next(it), next(it)
    w_gate, w_value, w_state, w_step, w_out = (next(it) for _ in range(5))
    taps_v, taps_s, heads_p, gain_in = (next(it) for _ in range(4))
    gate_ref, vin_ref, cv_ref, y_ref, sin_ref, cs_ref, dt_ref, hs_ref = (next(it) for _ in range(8))
    if not fresh:
        dh_c, av_c, as_c, ah_c = (next(it) for _ in range(4))
    for _ in range(n_skip):
        next(it)
    dgate_out, dval_out, dst_out, dstep_out = (next(it) for _ in range(4))
    keep, send = next(it), next(it)
    d_state, acc_v, acc_s, acc_h = (next(it) for _ in range(4))
    acc, dst_s, db_s, dc_s, vbuf, sbuf = (next(it) for _ in range(6))
    b_s, c_s, ct_s, st_s, step_s, cum_s, cumt_s, dcum_s, dstep_s, end_s = (
        next(it) for _ in range(10)
    )
    bufs = [next(it) for _ in range(5)]
    fetch = Fetch(l, (w_gate, w_value, w_out, w_state, w_step), bufs, next(it))

    i, g = pl.program_id(0), pl.program_id(1)
    core = scal[0]
    bias, decay_log = heads_p[0:1, :], heads_p[1:2, :]

    @pl.when(g == 0)
    def _():
        @pl.when(i == 0)
        def _():
            fetch.start((2, 0, 1), False)
            if fresh:
                d_state[...] = jnp.zeros_like(d_state)
                acc_v[...] = jnp.zeros_like(acc_v)
                acc_s[...] = jnp.zeros_like(acc_s)
                acc_h[...] = jnp.zeros_like(acc_h)
            else:
                d_state[...] = dh_c[...]
                acc_v[...] = av_c[...]
                acc_s[...] = as_c[...]
                acc_h[...] = ah_c[...]

        cs = cs_ref[...]
        states = cs * sigmoid(cs)
        b_val, c_val = states[:, :LANES], states[:, LANES:]
        b_s[...] = b_val.astype(BF16)
        c_s[...] = c_val.astype(BF16)
        ct_s[...] = c_val.T.astype(BF16)
        st_s[...] = nt(b_s[...], c_s[...])
        step = softplus(dt_ref[...] + bias)
        cum = -exact(triangle(True).astype(F32), step * jnp.exp(decay_log))
        step_s[...] = step
        cum_s[...] = cum
        cumt_s[...] = cum.T
        acc[...] = jnp.zeros_like(acc)
        dst_s[...] = jnp.zeros_like(dst_s)
        db_s[...] = jnp.zeros_like(db_s)
        dc_s[...] = jnp.zeros_like(dc_s)
        dcum_s[...] = jnp.zeros_like(dcum_s)
        dstep_s[...] = jnp.zeros_like(dstep_s)
        end_s[...] = jnp.zeros_like(end_s)

    scale, coef = rows_ref[:, 0:1], rows_ref[:, 1:2]
    skip = skip_row(heads_p, g)

    @pl.when(i == 0)
    def _():
        fetch.grouped(2, g).wait()

    d_go = nn(gb_ref[...], bufs[2][g])
    cv = cv_ref[...]
    sig_v = sigmoid(cv)
    val = cv * sig_v
    gate = gate_ref[...].astype(F32)
    sig_g = sigmoid(gate)
    silu_g = gate * sig_g
    y = y_ref[...]
    mixed = y + skip * val
    gated = mixed * silu_g
    normed_gate = gated * scale
    acc_v[g, 5:6, :] += col_sum(d_go * normed_gate)
    d_gated = scale * (d_go * gain_in[...]) - gated * coef
    d_gate = (d_gated * mixed * (sig_g * (1.0 + gate * (1.0 - sig_g)))).astype(BF16)
    dgate_out[...] = d_gate
    d_y = d_gated * silu_g
    acc_v[g, 6:7, :] += col_sum(d_y * val)
    d_y_b = d_y.astype(BF16)
    d_y_r = d_y_b.astype(F32)

    cum_g = to_group(cum_s[...], g)
    step_g = to_group(step_s[...], g)
    cum_e = spread(cum_g)
    step_e = spread(step_g)
    scaled = step_e * val
    scaled_b = scaled.astype(BF16)
    scaled_r = scaled_b.astype(F32)
    causal_t = triangle(False)
    tiles = []
    for q in range(GC // LANES):
        tile = jnp.zeros((Q, LANES), F32)
        x_tile = scaled_b[:, q * LANES : (q + 1) * LANES]
        g_tile = d_y_b[:, q * LANES : (q + 1) * LANES]
        for parity in range(2):
            j = 2 * q + parity
            gaps = cumt_s[pl.ds(g * HG + j, 1), :] - cum_g[:, j : j + 1]
            weights = jnp.exp(jnp.where(causal_t, gaps, -1e30))
            mix = (st_s[...] * weights).astype(BF16)
            part = head_part(g_tile, parity)
            tile = tile + nn(mix, part)
            dst_s[...] += nt(x_tile, part) * weights
        tiles.append(tile)
    d_x = jnp.concatenate(tiles, axis=1)
    end = cum_e[Q - 1 : Q, :]
    exp_end = jnp.exp(end)
    to_end = jnp.exp(end - cum_e)
    h_enter = hs_ref[...]
    d_out = d_state[g]
    d_out_b = d_out.astype(BF16)
    d_across = (d_y * jnp.exp(cum_e)).astype(BF16)
    dc_s[...] += nt(d_across, h_enter.astype(BF16))
    db_s[...] += nt((scaled * to_end).astype(BF16), d_out_b)
    d_x_end = to_end * nn(b_s[...], d_out_b)
    d_state[g] = nn(ct_s[...], d_across) + exp_end * d_out
    end_s[...] = gather_heads(
        end_s[...],
        jnp.broadcast_to(col_sum(scaled_r * d_x_end) + exp_end * col_sum(h_enter * d_out), (8, GC)),
        g,
    )
    d_x = d_x + d_x_end
    dcum_s[...] = gather_heads(dcum_s[...], d_y_r * y - scaled_r * d_x, g)
    dstep_s[...] = gather_heads(dstep_s[...], val * d_x, g)
    d_val = skip * d_y + step_e * d_x
    d_cv = d_val * (sig_v * (1.0 + cv * (1.0 - sig_v)))
    vbuf[0:Q, :] = d_cv
    vbuf[Q : Q + 8, :] = acc_v[g, 8:16, :]
    acc_v[g, 8:16, :] = d_cv[0:8, :]
    v_in = vin_ref[...].astype(F32)
    d_vin = taps_v[3:4, :] * d_cv
    acc_v[g, 3:4, :] += col_sum(v_in * d_cv)
    acc_v[g, 4:5, :] += col_sum(d_cv)
    for k in range(3):
        shifted = vbuf[3 - k : 3 - k + Q, :]
        d_vin = d_vin + taps_v[k : k + 1, :] * shifted
        acc_v[g, k : k + 1, :] += col_sum(v_in * shifted)
    d_vin_b = d_vin.astype(BF16)
    dval_out[...] = d_vin_b

    @pl.when(i == 0)
    def _():
        fetch.grouped(0, g).wait()
        fetch.grouped(1, g).wait()

    acc[...] += nt(d_gate, bufs[0][g]) + nt(d_vin_b, bufs[1][g])

    @pl.when(g == pl.num_programs(1) - 1)
    def _():
        decay = jnp.exp(decay_log)
        step = step_s[...]
        d_log = exact(triangle(False).astype(F32), dcum_s[...]) + end_s[0:1, :]
        acc_h[1:2, :] += col_sum(d_log * step) * (-decay)
        d_step = (dstep_s[...] - decay * d_log) * sigmoid(dt_ref[...] + bias)
        acc_h[0:1, :] += col_sum(d_step)
        d_step_b = d_step.astype(BF16)
        dstep_out[...] = d_step_b
        d_scores = dst_s[...]
        d_b = db_s[...] + nn(d_scores.astype(BF16), c_s[...])
        d_c = dc_s[...] + nn(d_scores.T.astype(BF16), b_s[...])
        cs = cs_ref[...]
        sig_s = sigmoid(cs)
        d_cs = jnp.concatenate([d_b, d_c], axis=1) * (sig_s * (1.0 + cs * (1.0 - sig_s)))
        sbuf[0:Q, :] = d_cs
        sbuf[Q : Q + 8, :] = acc_s[8:16, :]
        acc_s[8:16, :] = d_cs[0:8, :]
        s_in = sin_ref[...].astype(F32)
        d_sin = taps_s[3:4, :] * d_cs
        acc_s[3:4, :] += col_sum(s_in * d_cs)
        acc_s[4:5, :] += col_sum(d_cs)
        for k in range(3):
            shifted = sbuf[3 - k : 3 - k + Q, :]
            d_sin = d_sin + taps_s[k : k + 1, :] * shifted
            acc_s[k : k + 1, :] += col_sum(s_in * shifted)
        d_sin_b = d_sin.astype(BF16)
        dst_out[...] = d_sin_b

        @pl.when(i == 0)
        def _():
            fetch.single(3).wait()
            fetch.single(4).wait()

        acc[...] += nt(d_sin_b, bufs[3][...]) + nt(d_step_b, bufs[4][...])
        split_halves(acc, keep, send, core, half)


def weight_kernel(half, bit, pieces, scal, a_ref, *refs):
    ds = refs[:pieces]
    at = 0
    if bit is None:
        out = refs[-1]
        for d in ds:
            out[:, at : at + d.shape[1]] = tn(a_ref[...], d[...]).astype(BF16)
            at += d.shape[1]
        return
    keep, send, buf = refs[-3:]
    for d in ds:
        buf[:, at : at + d.shape[1]] = tn(a_ref[...], d[...])
        at += d.shape[1]
    mine = scal[bit]
    for m in range(buf.shape[0] // (2 * half)):
        own = pl.multiple_of(2 * half * m + half * mine, 8)
        other = pl.multiple_of(2 * half * m + half * (1 - mine), 8)
        keep[half * m : half * m + half, :] = buf[pl.ds(own, half), :].astype(BF16)
        send[half * m : half * m + half, :] = buf[pl.ds(other, half), :].astype(BF16)


def layer_specs(l):
    return [pl.BlockSpec(memory_space=pl.ANY)] * 5 + [
        pl.BlockSpec((None, 5, GC), lambda i, g: (l, 0, g)),
        pl.BlockSpec((None, 5, 2 * LANES), lambda i, g: (l, 0, 0)),
        pl.BlockSpec((None, 8, LANES), lambda i, g: (l, 0, 0)),
        pl.BlockSpec((None, 1, GC), lambda i, g: (l, 0, g)),
    ]


class Far:
    def __init__(self, value):
        self.value = value


class Call:
    def __init__(self):
        self.in_specs, self.args, self.out_specs, self.out_shape = [], [], [], []
        self.aliases, self.tail = {}, []

    def take(self, spec, arg, stay=False):
        self.in_specs.append(spec)
        self.args.append(pltpu.with_memory_space_constraint(arg, pltpu.HBM) if stay else arg)

    def give(self, spec, dims, dtype=F32, into=None, keep=False):
        if into is not None:
            self.tail.append((into, len(self.out_specs)))
        self.out_specs.append(spec)
        kind = pltpu.HBM if keep else jax.ShapeDtypeStruct
        self.out_shape.append(kind(dims, dtype))

    def run(self, kernel, grid, scratch, after, micros, name):
        for arg, out in self.tail:
            self.aliases[len(self.args)] = out
            self.take(pl.BlockSpec(memory_space=pl.ANY), arg)
        for arg in after:
            stay = isinstance(arg, Far)
            self.take(pl.BlockSpec(memory_space=pl.ANY), arg.value if stay else arg, stay)
        return pl.pallas_call(
            functools.partial(kernel, len(self.tail) + len(after)),
            grid=grid,
            in_specs=self.in_specs,
            out_specs=self.out_specs,
            out_shape=self.out_shape,
            scratch_shapes=scratch,
            input_output_aliases=self.aliases,
            compiler_params=pltpu.CompilerParams(
                dimension_semantics=("arbitrary",) * len(grid),
                vmem_limit_bytes=(VMEM_LIMIT if name.startswith("layer") else VMEM_SMALL),
            ),
            cost_estimate=pl.CostEstimate(
                flops=int(micros * 1.1e9), bytes_accessed=1_000_000, transcendentals=0
            ),
            name=name,
        )(*self.args)


def full(dims, count):
    return pl.BlockSpec(dims, lambda *at: (0,) * count)


def smem():
    return pl.BlockSpec(memory_space=pltpu.SMEM)


def forward_call(l, chunk, chunks, half, inner, rows_all, scal, hid_prev, halves, halves_at, gains, weights, carry, filled, after):
    first, fresh = hid_prev is None, carry is None
    width = weights[0].shape[1]
    groups = weights[0].shape[2] // GC
    cols = groups * GC
    rows = chunks * Q

    def block(h, w, at=chunk):
        return pl.BlockSpec((h, w), lambda i, g: (at + i, 0))

    def grouped(h, w, at=chunk):
        return pl.BlockSpec((h, w), lambda i, g: (at + i, g))

    call = Call()
    call.take(smem(), scal)
    if not first:
        call.take(block(Q, width), hid_prev, stay=True)
    for term in halves:
        call.take(block(Q // 4 if first else Q // 2, term.shape[1], halves_at), term, stay=first)
    call.take(full(gains.shape, 2), gains)
    for k, (spec, arg) in enumerate(zip(layer_specs(l), weights)):
        call.take(spec, arg, stay=k < 5)
    carry_shapes = [(groups, LANES, GC), (groups, 8, GC), (8, 2 * LANES)]
    if not fresh:
        for dims, arg in zip(carry_shapes, carry):
            call.take(full(dims, len(dims)), arg)
    into = filled if filled is not None else (None,) * 3
    call.give(pl.BlockSpec(memory_space=pl.ANY), (rows_all, width), F32, into[0], keep=True)
    call.give(pl.BlockSpec(memory_space=pl.ANY), (rows_all, width), BF16, into[1], keep=True)
    call.give(grouped(Q, GC), (rows_all, cols), BF16, into[2], keep=True)
    if not first:
        call.give(block(Q, width + LANES, 0), (rows, width + LANES), BF16, keep=True)
    call.give(grouped(Q, GC, 0), (rows, cols), BF16, keep=True)
    call.give(grouped(Q, GC, 0), (rows, cols), BF16, keep=True)
    call.give(grouped(Q, GC, 0), (rows, cols), keep=True)
    call.give(grouped(Q, GC, 0), (rows, cols), keep=True)
    call.give(block(Q, 2 * LANES, 0), (rows, 2 * LANES), BF16, keep=True)
    call.give(block(Q, 2 * LANES, 0), (rows, 2 * LANES), keep=True)
    call.give(block(Q, LANES, 0), (rows, LANES), keep=True)
    call.give(
        pl.BlockSpec((None, None, LANES, GC), lambda i, g: (i, g, 0, 0)),
        (chunks, groups, LANES, GC),
        keep=True,
    )
    for dims in carry_shapes:
        call.give(full(dims, len(dims)), dims)
    for dtype in (F32, BF16):
        call.give(block(Q // 2, width + LANES, 0), (rows // 2, width + LANES), dtype)
    scratch = [
        pltpu.VMEM((Q, width + LANES), F32),
        pltpu.VMEM((Q, width + LANES), F32),
        pltpu.VMEM((Q, LANES), F32),
        pltpu.VMEM((Q + 8, GC), F32),
        pltpu.VMEM((Q + 8, 2 * LANES), F32),
        pltpu.VMEM((Q, LANES), BF16),
        pltpu.VMEM((Q, LANES), BF16),
        pltpu.VMEM((LANES, Q), BF16),
        pltpu.VMEM((Q, Q), F32),
        pltpu.VMEM((Q, LANES), F32),
        pltpu.VMEM((Q, LANES), F32),
        pltpu.VMEM((LANES, Q), F32),
        pltpu.VMEM((Q, width), BF16),
        pltpu.SemaphoreType.DMA((2,)),
    ] + fetch_scratch(width, groups)

    def kernel(n_skip, *refs):
        forward_kernel(first, fresh, n_skip, l, half, chunk * Q, inner, *refs)

    outs = call.run(kernel, (chunks, groups), scratch, after, 12 * chunks, "layer_forward")
    outs = list(outs)
    below = None if first else outs.pop(3)
    return tuple(outs[:3]), below, tuple(outs[3:11]), tuple(outs[11:14]), outs[14], outs[15]


def norm_call(l, top, bottom, chunk, chunks, half, inner, scal, hid, lead, lows, branch, gains, gain_c, filled, after):
    rows_all, width = hid.shape
    fresh = gain_c is None

    def block(h, w, at=chunk * (Q // R)):
        return pl.BlockSpec((h, w), lambda i: (at + i, 0))

    call = Call()
    call.take(smem(), scal)
    call.take(block(R, width), hid, stay=True)
    call.take(block(R, width), lead, stay=True)
    if not top:
        for side in lows:
            call.take(block(R // 2, width, 0), side)
    for side in branch:
        call.take(block(R // 2 if top else R, width + LANES, 0), side, stay=not top)
    call.take(full(gains.shape, 2), gains)
    if not fresh:
        call.take(full((8, width), 2), gain_c)
    into = filled if filled is not None else (None,) * 5
    if top:
        call.give(block(R, width), (rows_all, width), BF16, into[4], keep=True)
    part = 2 if bottom else 1
    call.give(block(R // part, width), (rows_all // part, width), F32, into[0], keep=True)
    call.give(block(R, width), (rows_all, width), BF16, into[1], keep=True)
    call.give(block(R, width), (rows_all, width), BF16, into[2], keep=True)
    call.give(block(R, LANES), (rows_all, LANES), F32, into[3])
    call.give(full((8, width), 2), (8, width))
    scratch = [pltpu.VMEM((R, width + LANES), F32), pltpu.VMEM((R, width), F32)]

    def kernel(n_skip, *refs):
        norm_kernel(top, bottom, fresh, n_skip, l, half, chunk * Q, inner, *refs)

    outs = call.run(kernel, (chunks * (Q // R),), scratch, after, 12 * chunks, "norm_backward")
    result = None
    if top:
        result, outs = outs[0], outs[1:]
    return tuple(outs[:4]) + (result,), outs[4]


def backward_call(l, chunk, chunks, half, scal, gb, rows_f, weights, saved, carry, filled, after):
    width = weights[0].shape[1]
    groups = weights[0].shape[2] // GC
    cols = groups * GC
    rows, rows_all = chunks * Q, gb.shape[0]
    fresh = carry is None

    def block(h, w, at=chunk):
        return pl.BlockSpec((h, w), lambda i, g: (at + chunks - 1 - i, 0))

    def grouped(h, w, at=chunk):
        return pl.BlockSpec((h, w), lambda i, g: (at + chunks - 1 - i, g))

    call = Call()
    call.take(smem(), scal)
    call.take(block(Q, width), gb, stay=True)
    call.take(block(Q, LANES), rows_f)
    for k, (spec, arg) in enumerate(zip(layer_specs(l), weights)):
        call.take(spec, arg, stay=k < 5)
    specs = [
        grouped(Q, GC, 0),
        grouped(Q, GC, 0),
        grouped(Q, GC, 0),
        grouped(Q, GC, 0),
        block(Q, 2 * LANES, 0),
        block(Q, 2 * LANES, 0),
        block(Q, LANES, 0),
        pl.BlockSpec((None, None, LANES, GC), lambda i, g: (chunks - 1 - i, g, 0, 0)),
    ]
    for spec, arg in zip(specs, saved):
        call.take(spec, arg, stay=True)
    carry_shapes = [(groups, LANES, GC), (groups, 16, GC), (16, 2 * LANES), (8, LANES)]
    if not fresh:
        for dims, arg in zip(carry_shapes, carry):
            call.take(full(dims, len(dims)), arg)
    into = filled if filled is not None else (None,) * 4
    call.give(grouped(Q, GC), (rows_all, cols), BF16, into[0], keep=True)
    call.give(grouped(Q, GC), (rows_all, cols), BF16, into[1], keep=True)
    call.give(block(Q, 2 * LANES), (rows_all, 2 * LANES), BF16, into[2], keep=True)
    call.give(block(Q, LANES), (rows_all, LANES), BF16, into[3], keep=True)
    for dtype in (F32, BF16):
        call.give(block(Q // 2, width, 0), (rows // 2, width), dtype)
    for dims in carry_shapes:
        call.give(full(dims, len(dims)), dims)
    scratch = [
        pltpu.VMEM((Q, width), F32),
        pltpu.VMEM((Q, Q), F32),
        pltpu.VMEM((Q, LANES), F32),
        pltpu.VMEM((Q, LANES), F32),
        pltpu.VMEM((Q + 8, GC), F32),
        pltpu.VMEM((Q + 8, 2 * LANES), F32),
        pltpu.VMEM((Q, LANES), BF16),
        pltpu.VMEM((Q, LANES), BF16),
        pltpu.VMEM((LANES, Q), BF16),
        pltpu.VMEM((Q, Q), F32),
        pltpu.VMEM((Q, LANES), F32),
        pltpu.VMEM((Q, LANES), F32),
        pltpu.VMEM((LANES, Q), F32),
        pltpu.VMEM((Q, LANES), F32),
        pltpu.VMEM((Q, LANES), F32),
        pltpu.VMEM((8, LANES), F32),
    ] + fetch_scratch(width, groups)

    def kernel(n_skip, *refs):
        backward_kernel(fresh, n_skip, l, half, *refs)

    outs = call.run(kernel, (chunks, groups), scratch, after, 16 * chunks, "layer_backward")
    return tuple(outs[:4]), outs[4], outs[5], tuple(outs[6:])


def weight_call(a, ds, piece, scal, bit, after):
    tokens, width = a.shape
    total = sum(d.shape[1] for d in ds)
    unit = piece * (bit or 1)
    step = 2 * unit
    while step < 384 and width % (2 * step) == 0:
        step *= 2
    call = Call()
    call.take(smem(), scal)
    call.take(pl.BlockSpec((tokens, step), lambda r: (0, r)), a, stay=True)
    for d in ds:
        call.take(full(d.shape, 2), d, stay=True)
    parts = 1 if bit is None else 2
    for _ in range(parts):
        call.give(pl.BlockSpec((step // parts, total), lambda r: (r, 0)), (width // parts, total), BF16, keep=True)
    scratch = [] if bit is None else [pltpu.VMEM((step, total), F32)]

    def kernel(n_skip, *refs):
        weight_kernel(unit, None if bit is None else place_of(bit), len(ds), *refs)

    return call.run(kernel, (width // step,), scratch, after, total // 128, "weight_grad")


def pack_call(rows, wide, moves, after):
    call = Call()
    for src, _, _ in moves:
        call.take(pl.BlockSpec(memory_space=pltpu.VMEM), src)
    call.give(pl.BlockSpec(memory_space=pltpu.VMEM), (rows, wide))

    def kernel(n_skip, *refs):
        out = refs[-1]
        out[...] = jnp.zeros_like(out)
        for ref, (_, index, at) in zip(refs, moves):
            piece = ref[index]
            if piece.shape[1] <= wide:
                out[at : at + piece.shape[0], : piece.shape[1]] = piece
            else:
                for m in range(piece.shape[1] // wide):
                    out[at + m : at + m + 1, :] = piece[:, m * wide : (m + 1) * wide]

    return call.run(kernel, (), [], after, 2, "pack_small")[0]


def sum_call(a, b, after):
    call = Call()
    for arg in (a, b):
        call.take(pl.BlockSpec(memory_space=pltpu.VMEM), arg)
    call.give(pl.BlockSpec(memory_space=pltpu.VMEM), a.shape)

    def kernel(n_skip, x, y, *refs):
        refs[-1][...] = x[...] + y[...]

    return call.run(kernel, (), [], after, 1, "sum_small")[0]


def take_call(value, index, after):
    call = Call()
    call.take(smem(), index)
    call.take(pl.BlockSpec(memory_space=pltpu.VMEM), value)
    call.give(pl.BlockSpec(memory_space=pltpu.VMEM), value.shape, value.dtype)

    def kernel(n_skip, at, src, *refs):
        for k in range(value.shape[0]):
            refs[-1][k] = src[at[k]]

    return call.run(kernel, (), [], after, 2, "take_parts")[0]


def touch_call(value, after):
    call = Call()
    call.give(pl.BlockSpec(memory_space=pl.ANY), value.shape, value.dtype, value)

    def kernel(n_skip, *refs):
        pass

    return call.run(kernel, (), [], after, 1, "touch")[0]


class Butterfly:
    def __init__(self, value, steps):
        self.value, self.steps = value, list(steps)
        self.send()

    def send(self):
        if self.steps:
            self.came = swap(self.value, *self.steps.pop(0))
        else:
            self.came = None

    def step(self, after):
        self.value = sum_call(self.value, self.came, after)
        self.send()
        return self.value


def pairs(axis, bit):
    return [(i, i ^ bit) for i in range(lax.axis_size(axis))]


def swap(value, axis, bit):
    return lax.ppermute(value, axis, pairs(axis, bit))


def sum_pairs(value, axis, bit):
    return value + swap(value, axis, bit)


def place_of(bit):
    return 1 + bit.bit_length() + (bit >= 4)


class Scatter:
    def __init__(self, keep, send, piece, order):
        self.keep, self.recv, self.piece = keep, swap(send, "dp", order[0]), piece
        self.order, self.left = list(order[1:]), sorted(order[1:])

    def step(self, scal, after):
        bit = self.order.pop(0)
        unit = self.piece << self.left.index(bit)
        self.left.remove(bit)
        self.keep, send = scatter_call(self.keep, self.recv, unit, place_of(bit), scal, after)
        self.recv = swap(send, "dp", bit)
        return Far(send)


def finish_call(items, after):
    call = Call()
    count = 0
    for scatter, upper, parts in items:
        rows = scatter.keep.shape[0]
        for arg in (scatter.keep, scatter.recv):
            call.take(pl.BlockSpec(arg.shape, lambda r: (0, 0)), arg, stay=True)
        for wide, at in parts:
            call.take(pl.BlockSpec((rows, wide), lambda r, j=at // wide: (0, j)), upper, stay=True)
            call.give(pl.BlockSpec((2, rows, wide), lambda r: (0, 0, 0)), (2, rows, wide))
            count += 1

    def kernel(n_skip, *refs):
        it, out = iter(refs), iter(refs[len(refs) - count :])
        for _, _, parts in items:
            a, b, at = next(it), next(it), 0
            for wide, _ in parts:
                cols = slice(at, at + wide)
                dst = next(out)
                dst[0] = a[:, cols].astype(F32) + b[:, cols].astype(F32)
                dst[1] = next(it)[...].astype(F32)
                at += wide

    return call.run(kernel, (1,), [], after, 3, "finish")


def own_part(rows, half, place):
    parts = rows.reshape(-1, 2, half // 2, rows.shape[1])
    return lax.dynamic_index_in_dim(parts, place, axis=1, keepdims=False).reshape(-1, rows.shape[1])


def add_call(keep, recv, width, after):
    rows, wide = keep.shape
    call = Call()
    spec = pl.BlockSpec((rows // 2, wide), lambda r: (r, 0))
    call.take(spec, keep)
    call.take(spec, recv)
    call.give(spec, (rows, wide), BF16)

    def kernel(n_skip, a, b, *refs):
        out = refs[-1]
        total = a[...] + b[...].astype(F32)
        out[:, :width] = total[:, :width].astype(BF16)
        if wide > width:
            column = total[:, width : width + 1] + total[:, width + P_SIZE : width + P_SIZE + 1]
            out[:, width:] = two_terms(column).astype(BF16)

    return call.run(kernel, (2,), [], after, 2, "add_pair")[0]


def add_quarter_call(keep, recv, half, scal, after):
    rows, wide = keep.shape
    unit = half // 2
    call = Call()
    call.take(smem(), scal)
    for arg in (keep, recv):
        call.take(pl.BlockSpec(memory_space=pltpu.VMEM), arg)
    call.give(pl.BlockSpec(memory_space=pltpu.VMEM), (rows // 2, wide))
    call.give(pl.BlockSpec(memory_space=pltpu.VMEM), (rows // 2, wide), BF16)

    def kernel(n_skip, place_ref, a, b, *refs):
        mine, other, buf, came = refs[-4:]
        place = place_ref[4]
        came[...] = b[...].astype(F32)
        for m in range(rows // half):
            for dst, side in ((mine, place), (buf, 1 - place)):
                at = pl.multiple_of(half * m + unit * side, 8)
                dst[unit * m : unit * m + unit, :] = a[pl.ds(at, unit), :] + came[pl.ds(at, unit), :]
        other[...] = buf[...].astype(BF16)

    scratch = [pltpu.VMEM((rows // 2, wide), F32), pltpu.VMEM((rows, wide), F32)]
    return call.run(kernel, (), scratch, after, 2, "add_quarter")


def last_call(mine, other, d_hid, x_parts, chunk, half, scal, gains, gain_c, filled, after):
    rows, wide = mine.shape
    unit = half // 2
    fresh = gain_c is None
    call = Call()
    call.take(smem(), scal)
    part = pl.BlockSpec((rows, wide), lambda r: (0, 0))
    whole = pl.BlockSpec((2 * rows, wide), lambda r: (chunk, 0))
    x_part = pl.BlockSpec((rows, wide), lambda r: (max(chunk - 1, 0), 0))
    for spec, arg in ((part, mine), (part, other), (whole, d_hid), (x_part, x_parts[min(chunk, 1)][0])):
        call.take(spec, arg, stay=spec is whole or spec is x_part)
    call.take(full(gains.shape, 2), gains)
    if not fresh:
        call.take(full((8, wide), 2), gain_c)
    call.give(pl.BlockSpec((rows, wide), lambda r: (chunk, 0)), (d_hid.shape[0] // 2, wide), BF16, filled, keep=True)
    call.give(full((8, wide), 2), (8, wide))

    def kernel(n_skip, place_ref, a, b, dh_ref, x_ref, gain_ref, *refs):
        out, gain_acc, x_q, dh_q = refs[-4:]
        place = place_ref[4]
        x_q[...] = x_ref[...].astype(F32)
        for m in range(rows // unit):
            at = pl.multiple_of(half * m + unit * place, 8)
            dst = slice(unit * m, unit * m + unit)
            token = chunk * Q + (2 * half) * m + half * place_ref[0] + unit * place
            token = token + lax.broadcasted_iota(jnp.int32, (unit, 1), 0)
            x_q[dst, :] = jnp.where(token < place_ref[1], x_q[dst, :], 0.0)
            dh_q[dst, :] = jnp.where(token < place_ref[1], dh_ref[pl.ds(at, unit), :], 0.0)
        hid = x_q[...]
        r = lax.rsqrt(row_mean(hid * hid) + EPS)
        normed = hid * r
        upper = a[...] + b[...].astype(F32)
        gain_acc[...] = jnp.zeros_like(gain_acc) if fresh else refs[0][...]
        gain_acc[0:1, :] += col_sum(upper * normed)
        dn = upper * gain_ref[0:1, :]
        back = r * (dn - normed * row_mean(dn * normed))
        out[...] = (dh_q[...] + back).astype(BF16)

    scratch = [pltpu.VMEM((rows, wide), F32), pltpu.VMEM((rows, wide), F32)]
    return call.run(kernel, (1,), scratch, after, 4, "norm_last")


def scatter_call(keep, recv, unit, place_at, scal, after):
    rows, wide = keep.shape
    call = Call()
    call.take(smem(), scal)
    spec = pl.BlockSpec((2 * unit, wide), lambda r: (r, 0))
    call.take(spec, keep, stay=True)
    call.take(spec, recv, stay=True)
    for _ in range(2):
        call.give(pl.BlockSpec((unit, wide), lambda r: (r, 0)), (rows // 2, wide), BF16, keep=True)

    def kernel(n_skip, place_ref, a, b, *refs):
        own = place_ref[place_at]
        for dst, side in ((refs[-2], own), (refs[-1], 1 - own)):
            at = pl.ds(pl.multiple_of(unit * side, 16), unit)
            dst[...] = (a[at, :].astype(F32) + b[at, :].astype(F32)).astype(BF16)

    return call.run(kernel, (rows // (2 * unit),), [], after, 3, "add_scatter")


class Offload:
    def __init__(self, value):
        self.value = lax.psum_scatter(value, "dp", scatter_dimension=0, tiled=True)


class Sums:
    def __init__(self, width, half, scal):
        self.width, self.half, self.scal, self.open = width, half, scal, []

    def start(self, keep, send):
        self.open.insert(0, [keep, swap(send, "tensor", 1), None, None])

    def add(self, entry, after):
        keep, recv = entry[0], entry[1]
        own = add_call(keep, recv, self.width, after)
        other = swap(own, "tensor", 2)
        entry[2] = own
        entry[3] = (own, other, swap(own, "tensor", 1), swap(other, "tensor", 1))
        return own

    def add_quarter(self, entry, after):
        mine, other = add_quarter_call(entry[0], entry[1], self.half, self.scal, after)
        entry[2] = other
        entry[3] = (mine, swap(other, "tensor", 2))
        return other


def per_device(
    x_in,
    cotangent,
    lengths,
    deal_order,
    norm_gains,
    proj_gate,
    proj_value,
    proj_state,
    proj_step,
    proj_out,
    conv_value,
    conv_state,
    step_bias,
    decay_log,
    skip_gain,
    inner_gain,
):
    _, slot_len, width = cotangent.shape
    layers = proj_gate.shape[0]
    cols = proj_gate.shape[2]
    heads = step_bias.shape[1]
    inner = cols * lax.axis_size("tensor")
    dp = lax.axis_size("dp")
    half = x_in.shape[1] // 2
    piece = width // dp
    me = lax.axis_index("dp")
    core = lax.rem(lax.axis_index("tensor"), 2)
    length = jnp.take(lengths, lax.dynamic_index_in_dim(deal_order, me, keepdims=False))
    place = lax.axis_index("tensor") // 2
    bits = [1 << k for k in range(dp.bit_length() - 1)]
    parts = [lax.rem(me // bit, 2) for bit in bits]
    scal = jnp.stack([core, length] + parts[:2] + [place] + parts[2:]).astype(jnp.int32)

    quarter = half // 2
    x_own = lax.dynamic_slice_in_dim(x_in, core * half + place * quarter, quarter, axis=1)
    x_dealt = jnp.take(x_own, deal_order, axis=0)
    x_own = lax.all_to_all(x_dealt, "dp", split_axis=0, concat_axis=0, tiled=True)
    x_own = x_own.reshape(slot_len // 4, width)
    x_first, x_rest = x_own[: Q // 4], x_own[Q // 4 :]
    along = swap(x_first, "tensor", 2)
    x_parts = [(x_first, along, swap(x_first, "tensor", 1), swap(along, "tensor", 1))]
    x_rest_along, x_rest_pair = swap(x_rest, "tensor", 2), swap(x_rest, "tensor", 1)

    heads_p = jnp.pad(
        jnp.stack([step_bias, decay_log, skip_gain], axis=1), ((0, 0), (0, 5), (0, LANES - heads))
    )
    weights = (
        proj_gate,
        proj_value,
        proj_state,
        jnp.pad(proj_step, ((0, 0), (0, 0), (0, LANES - heads))),
        proj_out,
        conv_value,
        conv_state,
        heads_p,
        inner_gain[:, None, :],
    )
    cot = cotangent.reshape(slot_len, width)
    sums = Sums(width, half, scal)
    calls = slot_len // (Q * CHUNKS)

    def due(entries, prior):
        if len(entries) > 1 and entries[1][2] is None:
            entries_add(entries[1], [prior])
        return [entries[1][2]] if len(entries) > 1 else []

    entries_add = sums.add
    filled_f, saves, branches, belows = [], [], [], []
    prior = None
    for l in range(layers):
        carry, filled, save_l, branch_l = None, None, [], []
        for c in range(calls):
            if l == 0:
                if c == 1:
                    along = touch_call(x_rest_along, [prior])
                    x_parts.append((x_rest, along, x_rest_pair, swap(along, "tensor", 1)))
                lead = (None, x_parts[min(c, 1)], max(c - 1, 0))
            else:
                lead = (filled_f[l - 1][0], branches[l - 1][c][3], 0)
            after = due(sums.open, prior)
            if len(sums.open) > 2:
                after.append(sums.open[2][3][1])
            filled, below, saved, carry, keep, send = forward_call(
                l, c * CHUNKS, CHUNKS, half, inner, slot_len, scal, *lead, norm_gains, weights, carry, filled, after
            )
            prior = keep
            save_l.append(saved)
            sums.start(keep, send)
            branch_l.append(sums.open[0])
            belows.append((below,))
        filled_f.append(filled)
        saves.append(save_l)
        branches.append(branch_l)
    prior = sums.add(sums.open[1], [prior])

    swapped = [bits[1], bits[0]] + bits[2:]
    lows = [(None,) * 4] * calls
    filled_n = None
    smalls, g_outs, g_ins = [], [], []
    for l in reversed(range(layers)):
        top, bottom = l == layers - 1, l == 0
        order = list(range(calls)) if top else list(reversed(range(calls)))
        lead = cot if top else filled_n[0]
        hid = filled_f[l][0] if top else filled_f[l + 1][0]
        filled_n, gain_c = None, None
        for c in order:
            after = [prior] if c == order[0] else []
            if top and c == order[2]:
                after = [sums.add(sums.open[0], [gain_c])]
            filled_n, gain_c = norm_call(
                l, top, bottom, c * CHUNKS, CHUNKS, half, inner, scal, hid, lead, lows[c][3] if not top else None, branches[l][c][3] if top else belows[(l + 1) * calls + c], norm_gains, gain_c, filled_n, after
            )
        if top:
            result = filled_n[4]
        _, low_all, u_all = filled_f[l]
        carry, filled, new_lows = None, None, [None] * calls
        sums.open = []
        if bottom:
            out_keep, out_send = weight_call(filled_n[2], [u_all], piece, scal, bits[0], [])
            out = Scatter(out_keep, out_send, piece, bits)
            entries_add = sums.add_quarter
            last, gain_first = None, None
        else:
            out_send = weight_call(filled_n[2], [u_all], piece, scal, None, [])[0]
            out = Offload(out_send)
        g_outs.insert(0, out)
        prior = Far(out_send)
        for at, c in enumerate(reversed(range(calls))):
            after = due(sums.open, prior)
            if not sums.open:
                after = [Far(out_send)]
            if bottom:
                if at >= 3:
                    after.append(out.step(scal, [after[0]]))
                if at >= 2 and len(sums.open) > 2:
                    last, gain_first = last_call(
                        *sums.open[2][3], filled_n[0], x_parts, (c + 3) * CHUNKS, half, scal, norm_gains, gain_first, last, [prior]
                    )
                    after.append(gain_first)
            elif len(sums.open) > 2:
                after.append(sums.open[2][3][1])
            filled, keep, send, carry = backward_call(
                l, c * CHUNKS, CHUNKS, half, scal, filled_n[1], filled_n[3], weights, saves[l][c], carry, filled, after
            )
            prior = keep
            sums.start(keep, send)
            new_lows[c] = sums.open[0]
        lows = new_lows
        _, acc_v, acc_s, acc_h = carry
        smalls.insert(0, (acc_v, acc_s, acc_h, gain_c))
        d_gate, d_val, d_st, d_step = filled
        if not bottom:
            prior = sums.add(sums.open[1], [prior])
            prior = sums.add(sums.open[0], [prior])
            after = [prior, Far(out.value)]
            in_send = weight_call(low_all, [d_val, d_gate, d_st, d_step], piece, scal, None, after)[0]
            g_ins.insert(0, Offload(in_send))
            prior = Far(in_send)

    def finish_rows(entry, chunk, after):
        return last_call(
            *entry[3], filled_n[0], x_parts, chunk * CHUNKS, half, scal, norm_gains, gain_first, last, after
        )

    groups = cols // GC
    gain_rows = width // GC
    dp_steps = [("dp", bit) for bit in bits]
    prior = sums.add_quarter(sums.open[1], [prior])
    last, gain_first = finish_rows(sums.open[2], 2, [prior])
    per_layer = groups * 8 + 8 + 8 * ((gain_rows + 7) // 8)
    moves = []
    for l, (acc_v, _, acc_h, gain) in enumerate(smalls):
        for g in range(groups):
            moves.append((acc_v, (g, slice(0, 8)), l * per_layer + 8 * g))
        moves.append((acc_h, slice(0, 8), l * per_layer + 8 * groups))
        moves.append((gain, slice(0, 1), l * per_layer + 8 * groups + 8))
    small = Butterfly(pack_call(layers * per_layer, GC, moves, [gain_first]), dp_steps)
    prior = sums.add_quarter(sums.open[0], [small.value])
    prior = small.step([prior])
    val_keep, val_send = weight_call(low_all, [d_val], piece, scal, bits[0], [prior])
    val = Scatter(val_keep, val_send, piece, bits)
    last, gain_first = finish_rows(sums.open[1], 1, [Far(val_send)])
    prior = small.step([gain_first])
    last, gain_first = finish_rows(sums.open[0], 0, [prior])
    rows = 8 * layers
    moves = [(acc_s, slice(0, 8), 8 * l) for l, (_, acc_s, _, _) in enumerate(smalls)]
    moves.append((gain_first, slice(0, 1), rows))
    rest_small = Butterfly(
        pack_call(rows + 8 * ((gain_rows + 7) // 8), GC, moves, []),
        [("tensor", 1), ("tensor", 2)] + dp_steps,
    )
    misc_keep, misc_send = weight_call(low_all, [d_st, d_step], piece, scal, swapped[0], [rest_small.value])
    misc = Scatter(misc_keep, misc_send, piece, swapped)
    prior = rest_small.step([Far(misc_send)])
    while small.came is not None:
        prior = small.step([prior])
    gate_keep, gate_send = weight_call(low_all, [d_gate], piece, scal, swapped[0], [prior])
    gate = Scatter(gate_keep, gate_send, piece, swapped)
    grad_in = last.reshape(dp, quarter, width)
    returned = lax.all_to_all(grad_in, "dp", split_axis=0, concat_axis=0, tiled=True)
    places = jnp.arange(dp)
    inverse = jnp.sum(jnp.where(deal_order[None, :] == places[:, None], places[None, :], 0), axis=1)
    arrived = take_call(returned, inverse.astype(jnp.int32), [Far(gate_send)])
    prior = misc.step(scal, [arrived])
    prior = val.step(scal, [prior])
    while out.order:
        prior = out.step(scal, [prior])
    prior = rest_small.step([prior])

    def side_by_side(mine, theirs, first):
        return jnp.where(
            first == 0,
            jnp.concatenate([mine, theirs], axis=1),
            jnp.concatenate([theirs, mine], axis=1),
        )

    joined = side_by_side(arrived, swap(arrived, "tensor", 2), place)
    grad_x = side_by_side(joined, swap(joined, "tensor", 1), core)

    upper = g_ins[0].value
    while misc.order:
        prior = misc.step(scal, [prior])
    prior = gate.step(scal, [prior, joined])
    g_state, g_step, g_out = finish_call(
        [
            (misc, upper, [(2 * LANES, 2 * cols), (LANES, 2 * cols + 2 * LANES)]),
            (out, g_outs[1].value, [(cols, 0)]),
        ],
        [prior],
    )
    g_state = Butterfly(g_state.reshape(-1, 2 * LANES), [("tensor", 1), ("tensor", 2)])
    prior = val.step(scal, [g_step])
    prior = g_state.step([prior])
    prior = rest_small.step([prior])
    while gate.order:
        prior = gate.step(scal, [prior])
    while val.order:
        prior = val.step(scal, [prior])
    prior = g_state.step([prior, Far(grad_x)])
    g_state = g_state.value.reshape(layers, -1, 2 * LANES)
    g_value, g_gate = finish_call([(val, upper, [(cols, 0)]), (gate, upper, [(cols, cols)])], [prior])
    prior = Far(g_gate)
    while rest_small.came is not None:
        prior = rest_small.step([prior])
    small, rest_small = small.value, rest_small.value
    small = small.reshape(layers, per_layer, GC)
    v_sum = jnp.swapaxes(small[:, : groups * 8].reshape(layers, groups, 8, GC), 1, 2)
    v_sum = v_sum.reshape(layers, 8, cols)
    h_sum = small[:, groups * 8 : groups * 8 + 2, :heads]
    gain_sum = small[:, groups * 8 + 8 : groups * 8 + 8 + gain_rows].reshape(layers, width)
    s_sum = rest_small[:rows].reshape(layers, 8, GC)[:, :5]
    gain_first = rest_small[rows : rows + gain_rows].reshape(1, width)
    gain_own = lax.dynamic_slice_in_dim(
        jnp.concatenate([gain_first, gain_sum], axis=0), me * piece, piece, axis=1
    )

    skip_grad = v_sum[:, 6].reshape(layers, heads, P_SIZE).sum(axis=2)
    return (
        result[None],
        grad_x,
        gain_own,
        g_gate,
        g_value,
        g_state,
        g_step[:, :, :heads],
        g_out,
        v_sum[:, :5],
        s_sum,
        h_sum[:, 0],
        h_sum[:, 1],
        skip_grad,
        v_sum[:, 5],
    )


def solution(mesh):
    return jax.shard_map(
        per_device,
        mesh=mesh,
        in_specs=(
            P(None, "dp", None),
            P("dp", None, None),
            P(),
            P(),
            P(),
            P(None, None, "tensor"),
            P(None, None, "tensor"),
            P(),
            P(None, None, "tensor"),
            P(None, None, "tensor"),
            P(None, None, "tensor"),
            P(),
            P(None, "tensor"),
            P(None, "tensor"),
            P(None, "tensor"),
            P(None, "tensor"),
        ),
        out_specs=(
            P("dp", None, None),
            P(None, "dp", None),
            P(None, "dp"),
            P(None, "dp", "tensor"),
            P(None, "dp", "tensor"),
            P(None, "dp", None),
            P(None, "dp", "tensor"),
            P(None, "dp", "tensor"),
            P(None, None, "tensor"),
            P(),
            P(None, "tensor"),
            P(None, "tensor"),
            P(None, "tensor"),
            P(None, "tensor"),
        ),
        check_vma=False,
    )
```
